256 devices in a mesh: tgt: 64 (over x, z, core), rep: 4 (over y).
Axes of the slice: x: 4, y: 4, z: 8, core: 2. Of those that a mesh axis runs over, the one named last changes fastest.
Arguments:
- flux: bfloat16 [16384, 7808], P(('tgt', 'rep')), may hold values from 0.19921875 to 4
- ivar: bfloat16 [16384, 7808], P(('tgt', 'rep')), may hold values from 0.099609375 to 10
- row_target: int32 [16384], P(('tgt', 'rep')), may hold values from 0 to 8191, as said below
- start_w: float32 [8192, 64], P(('tgt', 'rep')), may hold values from 0.02 to 0.25
- start_h: float32 [64, 7808], P(None, 'tgt'), may hold values from 0.02 to 0.25
Outputs:
- activations: float32 [8192, 64], P(('tgt', 'rep'))
- templates: float32 [64, 7808], P(None, 'tgt')
The draws below stay inside these ranges and needn't reach their ends.
Inputs may be any that keep to these rules, and one draw needn't show every extreme that they name: `row_target`: row i lies on device d = i // 64; its target t is owned by device t // 32, which has the same index along rep as d, i.e. (t // 32) % 4 == d % 4. The rows of one device name targets of one owning device at most 2 times, and every device reaches 2 for some owner. A target may have several rows or none.
All inputs are finite; a program needn't handle non-finite values.
Results may differ from the reference program's by a relative error of at most 0.035.
Values may be sent and summed in bfloat16 or wider, within the bound.
No kernel may reach another device: no remote copies, remote signals or barrier semaphores. Data moves between devices by JAX's collectives and lax.ppermute only.
A program may use at most 64 MiB of HBM per device.

```python
import math
import jax
import jax.numpy as jnp
from jax import lax

PIX = 7808
RANK = 64
TGT_DEV = 32
ROWS_DEV = 64
SWEEPS = 2
TARGETS = 8192
ROWS = 16384
CAP = 2
N_TGT = 64
N_REP = 4


def draw_row_target(key, part):
    key = jax.random.fold_in(key, 7)
    device_count = N_TGT * N_REP
    pair_count = N_TGT // 2
    key_pair, key_forced, key_peer, key_shuffle, key_local = jax.random.split(key, 5)
    pair_share = jax.random.randint(key_pair, (device_count, pair_count), 0, CAP + 1)
    forced = jax.random.randint(key_forced, (device_count, 1), 0, pair_count)
    pair_share = jnp.where(jnp.arange(pair_count)[None, :] == forced, CAP, pair_share)
    row_counts = jnp.stack([pair_share, CAP - pair_share], axis=2).reshape(device_count, N_TGT)
    peer_order = jax.vmap(lambda sub: jax.random.permutation(sub, N_TGT))(jax.random.split(key_peer, device_count))
    row_counts = jnp.take_along_axis(row_counts, peer_order, axis=1)
    row_bounds = jnp.cumsum(row_counts, axis=1)
    position = jnp.arange(ROWS_DEV)
    peer_dev = jnp.sum((position[None, :, None] >= row_bounds[:, None, :]).astype(jnp.int32), axis=2)
    shuffle = jax.vmap(lambda sub: jax.random.permutation(sub, ROWS_DEV))(jax.random.split(key_shuffle, device_count))
    peer_dev = jnp.take_along_axis(peer_dev, shuffle, axis=1)
    local_row = jax.random.randint(key_local, (device_count, ROWS_DEV), 0, TGT_DEV)
    rep_index = jnp.arange(device_count) % N_REP
    owner_dev = peer_dev * N_REP + rep_index[:, None]
    return (owner_dev * TGT_DEV + local_row).reshape(-1).astype(jnp.int32)


def level_of(key, shape, cuts, smallest, top_value):
    gain = 1.0
    for dim, blocks in cuts:
        steps = jax.random.uniform(jax.random.fold_in(jax.random.fold_in(key, 6), dim), (blocks,), jnp.float32, smallest / len(cuts), top_value / len(cuts))
        gain = gain * jnp.repeat(jnp.exp(steps), shape[dim] // blocks).reshape((-1,) + (1,) * (len(shape) - 1 - dim))
    return gain


def setup_inputs(seed: int = 0) -> dict:
    keys = jax.random.split(jax.random.key(seed), 6)
    flux = jnp.clip(jnp.exp(math.log(4.0) - 2.9996462 * jax.random.uniform(keys[0], (ROWS, PIX), jnp.float32) ** level_of(keys[0], (ROWS, PIX), ((0, 256),), -0.2, 0.2)), 0.19921875, 4.0).astype(jnp.bfloat16)
    ivar = jnp.clip(jnp.exp(math.log(10.0) - 4.609084 * jax.random.uniform(keys[1], (ROWS, PIX), jnp.float32) ** level_of(keys[1], (ROWS, PIX), ((0, 256),), -0.2, 0.2)), 0.099609375, 10.0).astype(jnp.bfloat16)
    row_target = draw_row_target(jax.random.fold_in(keys[5], 71), 0)
    start_w = jnp.clip(0.02 + 0.23 * jax.random.uniform(keys[3], (TARGETS, RANK), jnp.float32) ** level_of(keys[3], (TARGETS, RANK), ((0, 256),), -0.2, 0.2), 0.02, 0.25)
    start_h = jnp.clip(0.02 + 0.23 * jax.random.uniform(keys[4], (RANK, PIX), jnp.float32) ** level_of(keys[4], (RANK, PIX), ((1, 64),), -0.2, 0.2), 0.02, 0.25)
    return dict(flux=flux, ivar=ivar, row_target=row_target, start_w=start_w, start_h=start_h)


PRIOR_IVAR = 0.5
EPSILON = 1e-6


def update_columns(activation, cross, gram):
    def column_step(index, current):
        gram_col = lax.dynamic_index_in_dim(gram, index, 1, keepdims=False)
        pivot = lax.dynamic_index_in_dim(gram_col, index, 0, keepdims=False)
        column = lax.dynamic_index_in_dim(current, index, 1, keepdims=False)
        wanted = lax.dynamic_index_in_dim(cross, index, 1, keepdims=False)
        fitted = jnp.dot(current, gram_col, precision=lax.Precision.HIGHEST)
        updated = jnp.maximum(column + (wanted - fitted) / (pivot + EPSILON), 0.0)
        return lax.dynamic_update_index_in_dim(current, updated, index, 1)
    return lax.fori_loop(0, activation.shape[1], column_step, activation)


def update_rows(templates, proj, gram):
    def row_step(index, current):
        gram_row = lax.dynamic_index_in_dim(gram, index, 0, keepdims=False)
        pivot = lax.dynamic_index_in_dim(gram_row, index, 0, keepdims=False)
        row_now = lax.dynamic_index_in_dim(current, index, 0, keepdims=False)
        wanted = lax.dynamic_index_in_dim(proj, index, 0, keepdims=False)
        fitted = jnp.dot(gram_row, current, precision=lax.Precision.HIGHEST)
        updated = jnp.maximum(row_now + (wanted - fitted) / (pivot + EPSILON), 0.0)
        return lax.dynamic_update_index_in_dim(current, updated, index, 0)
    return lax.fori_loop(0, templates.shape[0], row_step, templates)


def reference(flux, ivar, row_target, start_w, start_h):
    weighted = (ivar.astype(jnp.float32) * flux.astype(jnp.float32)).astype(jnp.bfloat16)
    numerator = jax.ops.segment_sum(weighted.astype(jnp.float32), row_target, num_segments=TARGETS)
    denominator = jax.ops.segment_sum(ivar.astype(jnp.float32), row_target, num_segments=TARGETS)
    coadd = (numerator / (denominator + PRIOR_IVAR)).astype(jnp.bfloat16)
    activation = start_w
    templates = start_h
    for sweep in range(SWEEPS):
        cross = jnp.dot(coadd, templates.astype(jnp.bfloat16).T, preferred_element_type=jnp.float32)
        hgram = jnp.dot(templates, templates.T, precision=lax.Precision.HIGHEST)
        activation = update_columns(activation, cross, hgram)
        proj = lax.dot_general(activation.astype(jnp.bfloat16), coadd, (((0,), (0,)), ((), ())), preferred_element_type=jnp.float32)
        wgram = jnp.dot(activation.T, activation, precision=lax.Precision.HIGHEST)
        templates = update_rows(templates, proj, wgram)
    return activation, templates
```

```python
import jax
import jax.numpy as jnp
from jax import lax
from jax.experimental import pallas as pl
from jax.experimental.pallas import tpu as pltpu
from jax.sharding import Mesh, PartitionSpec as P

SWEEPS = 2
PRIOR_IVAR = 0.5
EPSILON = 1e-06

NX, NZ, NC, NY = 4, 8, 2, 4
N_TGT = NX * NZ * NC
ROWS = 64
RANK = 64
PIX = 122
LANES = 128
TGT = ("x", "z", "c")
BF = jnp.bfloat16
F32 = jnp.float32
VMEM = pl.BlockSpec(memory_space=pltpu.VMEM)
SMEM = pl.BlockSpec(memory_space=pltpu.SMEM)
NT = (((1,), (1,)), ((), ()))
TN = (((0,), (0,)), ((), ()))


def call(body, outs, args, scratch=(), scalars=0):
    return pl.pallas_call(
        body,
        out_shape=outs,
        in_specs=[SMEM] * scalars + [VMEM] * (len(args) - scalars),
        out_specs=jax.tree.map(lambda _: VMEM, outs),
        scratch_shapes=list(scratch),
        compiler_params=pltpu.CompilerParams(vmem_limit_bytes=40 * 2**20),
    )(*args)


def pack_body(flux_ref, ivar_ref, extra_ref, send_ref, weighted_ref):
    weighted_ref[...] = (
        ivar_ref[...].astype(F32) * flux_ref[...].astype(F32)
    ).astype(BF)
    extra = extra_ref[...]
    for dev in range(N_TGT):
        span = slice(dev * PIX, dev * PIX + PIX)
        send_ref[dev, :, 0:PIX] = weighted_ref[:, span]
        send_ref[dev, :, PIX:LANES] = extra[:, 0:LANES - PIX]
        send_ref[dev, :, LANES:LANES + PIX] = ivar_ref[:, span]
        send_ref[dev, :, LANES + PIX:2 * LANES] = jnp.zeros((ROWS, LANES - PIX), BF)


def template_pair(templ_bf):
    none = jnp.zeros_like(templ_bf)
    return jnp.concatenate(
        [
            jnp.concatenate([templ_bf, none], axis=1),
            jnp.concatenate([none, templ_bf], axis=1),
        ],
        axis=0,
    )


def cross_block(core, block, spectra, pair, keep_ref, send_ref):
    part = lax.dot_general(spectra, pair, NT, preferred_element_type=F32)
    place = pl.ds(pl.multiple_of((block % 2) * 256, 256), 256)

    @pl.when(block // 2 == core)
    def _():
        keep_ref[place, :] = part

    @pl.when(block // 2 != core)
    def _():
        send_ref[place, :] = part


def coadd_body(core_ref, got_ref, templ_ref, spectra_ref, keep_ref, send_ref, low_ref, high_ref):
    lane = lax.broadcasted_iota(jnp.int32, (16, 2 * LANES), 1)
    row = lax.broadcasted_iota(jnp.int32, (16, 2 * LANES), 0)
    pick = jnp.where(lane == PIX + row, 1.0, 0.0)
    pick = jnp.where(row < 2, pick, 0.0).astype(BF)
    ids = lax.dot_general(pick, got_ref[...], NT, preferred_element_type=F32)
    high_ref[...] = jnp.broadcast_to(ids[0:1, :], high_ref.shape)
    low = ids[1:2, :].astype(jnp.int32)
    low_ref[...] = jnp.where(
        low == lax.broadcasted_iota(jnp.int32, low_ref.shape, 0), 1.0, 0.0
    ).astype(BF)
    inside = lax.broadcasted_iota(jnp.int32, (256, LANES), 1) < PIX
    pair = template_pair(templ_ref[...].astype(BF))

    def block_step(block, carry):
        for half in range(2):
            first = ((half * 4 + block) * 4).astype(F32)
            selector = jnp.concatenate(
                [
                    low_ref[...]
                    * jnp.where(high_ref[0:1, :] == first + float(i), 1.0, 0.0).astype(BF)
                    for i in range(4)
                ],
                axis=0,
            )
            sums = jnp.dot(selector, got_ref[...], preferred_element_type=F32)
            coadd = sums[:, 0:LANES] / (sums[:, LANES:] + PRIOR_IVAR)
            spectra_ref[
                pl.ds(pl.multiple_of(block * 256, 256), 256),
                half * LANES:(half + 1) * LANES,
            ] = jnp.where(inside, coadd, 0.0).astype(BF)
        spectra = spectra_ref[pl.ds(pl.multiple_of(block * 256, 256), 256), :]
        cross_block(core_ref[0], block, spectra, pair, keep_ref, send_ref)
        return carry

    lax.fori_loop(0, 4, block_step, 0)


def pack_gram(gram):
    turned = pltpu.roll(
        jnp.concatenate([gram[32:64, :], jnp.zeros((32, 64), F32)], axis=1), 64, 1
    )
    return jnp.concatenate([gram[0:32, :], jnp.zeros((32, 64), F32)], axis=1) + turned


def unpack_gram(packed):
    return jnp.concatenate([packed[:, 0:64], pltpu.roll(packed, 64, 1)[:, 0:64]], axis=0)


def descend(state, wanted, gram):
    eye = lax.broadcasted_iota(jnp.int32, (RANK, RANK), 0) == lax.broadcasted_iota(
        jnp.int32, (RANK, RANK), 1
    )
    pivot = jnp.sum(jnp.where(eye, gram, 0.0), axis=1, keepdims=True) + EPSILON
    inverse = 1.0 / pivot
    fitted = jnp.dot(
        gram, state, precision=lax.Precision.HIGHEST, preferred_element_type=F32
    )
    goal = state + (wanted - fitted) * inverse
    scaled = gram * inverse
    goals = [goal[8 * i:8 * i + 8, :] for i in range(8)]
    done = []
    for k in range(RANK):
        old = state[k:k + 1, :]
        new = jnp.maximum(goals[k // 8][k % 8:k % 8 + 1, :], 0.0)
        done.append(new)
        change = new - old
        for i in range(k // 8, 8):
            goals[i] = goals[i] - scaled[8 * i:8 * i + 8, k:k + 1] * change
    return jnp.concatenate(done, axis=0)


def pad_to(value, rows, lanes):
    if value.shape[1] < lanes:
        value = jnp.concatenate(
            [value, jnp.zeros((value.shape[0], lanes - value.shape[1]), F32)], axis=1
        )
    if value.shape[0] < rows:
        value = jnp.concatenate(
            [value, jnp.zeros((rows - value.shape[0], value.shape[1]), F32)], axis=0
        )
    return value


def activation_body(first, cross_ref, gram_ref, state_ref, new_ref, out_ref):
    cross = pad_to(jnp.sum(cross_ref[...], axis=0), LANES, LANES).T
    wanted = cross[0:64, :] + pltpu.roll(cross[64:128, :], 16, 1)
    gram = unpack_gram(jnp.sum(gram_ref[...], axis=0))
    if first:
        state = pad_to(state_ref[...], LANES, LANES).T[0:RANK, :]
    else:
        state = state_ref[...]
    updated = descend(state, wanted, gram)
    if first:
        new_ref[...] = updated
    else:
        new_ref[...] = pad_to(updated, LANES, LANES).T[0:32, 0:RANK]
    both = jnp.concatenate([updated, pltpu.roll(updated, LANES - 16, 1)], axis=0).T
    out_ref[...] = jnp.broadcast_to(both[0:16, :].astype(BF)[None], out_ref.shape)


def project_body(core_ref, own_ref, other_ref, spectra_ref, out_ref):
    core = core_ref[0]
    proj, gram = 0.0, 0.0
    for ref, at in ((own_ref, core), (other_ref, 1 - core)):
        rows = spectra_ref[pl.ds(pl.multiple_of(at * 512, 512), 512), :]
        proj += lax.dot_general(ref[...], rows, TN, preferred_element_type=F32)
        gram += lax.dot_general(ref[...], ref[...], TN, preferred_element_type=F32)
    out_ref[0:64, :] = proj[0:64, 0:LANES] + proj[64:128, LANES:]
    gram = gram[0:64, 0:64] + pltpu.roll(gram[64:128, :], 64, 1)[:, 0:64]
    out_ref[64:96, :] = pack_gram(gram)


def new_templates(part_refs, templ_ref):
    one, two, three, four = (ref[...] for ref in part_refs)
    total = (one + three) + (two + four)
    return descend(templ_ref[...], total[0:64, :], unpack_gram(total[64:96, :]))


def template_body(core_ref, a_ref, b_ref, c_ref, d_ref, templ_ref, spectra_ref, new_ref, keep_ref, send_ref, gram_ref):
    updated = new_templates((a_ref, b_ref, c_ref, d_ref), templ_ref)
    new_ref[...] = updated
    templ_bf = updated.astype(BF)
    gram_ref[...] = pack_gram(
        lax.dot_general(templ_bf, templ_bf, NT, preferred_element_type=F32)
    )
    pair = template_pair(templ_bf)
    for block in range(4):
        spectra = spectra_ref[block * 256:(block + 1) * 256, :]
        cross_block(core_ref[0], block, spectra, pair, keep_ref, send_ref)


def last_template_body(a_ref, b_ref, c_ref, d_ref, templ_ref, new_ref):
    updated = new_templates((a_ref, b_ref, c_ref, d_ref), templ_ref)
    new_ref[...] = updated[:, 0:PIX]


def first_gram_body(templ_ref, gram_ref):
    templ_bf = templ_ref[...].astype(BF)
    gram_ref[...] = pack_gram(
        lax.dot_general(templ_bf, templ_bf, NT, preferred_element_type=F32)
    )


def shift(value, axis, size, by):
    return lax.ppermute(value, axis, [(i, (i + by) % size) for i in range(size)])


def everywhere(part):
    part = part + shift(part, "c", NC, 1)
    part = (part + shift(part, "x", NX, 2)) + (shift(part, "x", NX, 1) + shift(part, "x", NX, 3))
    return lax.all_to_all(
        jnp.broadcast_to(part[None], (NZ, *part.shape)), "z", split_axis=0, concat_axis=0, tiled=True
    )


def sds(*shape, dtype=F32):
    return jax.ShapeDtypeStruct(shape, dtype)


def shards(flux, ivar, row_target, start_w, start_h):
    core = lax.axis_index("c").astype(jnp.int32).reshape(1)
    peer, local = row_target // 128, row_target % 32
    index = (local // 16) * 1024 + (peer % 2) * 512 + (peer // 2) * 16 + local % 16
    extra = jnp.pad(
        jnp.stack([index // 64, index % 64], axis=1).astype(BF), ((0, 0), (0, LANES - 2))
    )
    send = call(
        pack_body,
        sds(N_TGT, ROWS, 2 * LANES, dtype=BF),
        (flux, ivar, extra),
        scratch=[pltpu.VMEM(flux.shape, BF)],
    )
    got = lax.all_to_all(send, TGT, split_axis=0, concat_axis=0, tiled=True)
    templates = jnp.pad(start_h, ((0, 0), (0, LANES - PIX)))
    gram = everywhere(call(first_gram_body, sds(32, LANES), (templates,)))
    spectra, keep, away = call(
        coadd_body,
        (sds(1024, 2 * LANES, dtype=BF), sds(512, LANES), sds(512, LANES)),
        (core, got.reshape(N_TGT * ROWS, 2 * LANES), templates),
        scratch=[pltpu.VMEM((64, N_TGT * ROWS), BF), pltpu.VMEM((8, N_TGT * ROWS), F32)],
        scalars=1,
    )
    state = start_w
    for sweep in range(SWEEPS):
        cross = (keep + shift(away, "c", NC, 1)).reshape(32, 16, LANES)
        cross = lax.all_to_all(cross, ("x", "z"), split_axis=0, concat_axis=0, tiled=True)
        first = sweep == 0
        state, message = call(
            lambda *refs, first=first: activation_body(first, *refs),
            (sds(RANK, LANES) if first else sds(32, RANK), sds(32, 16, LANES, dtype=BF)),
            (cross, gram, state),
        )
        own = lax.all_to_all(message, ("x", "z"), split_axis=0, concat_axis=0, tiled=True)
        own = own.reshape(512, LANES)
        other = shift(own, "c", NC, 1)
        part = call(
            project_body, sds(96, LANES), (core, own, other, spectra), scalars=1
        )
        parts = (part, *(shift(part, "y", NY, by) for by in (1, 2, 3)))
        if first:
            templates, keep, away, gram = call(
                template_body,
                (sds(RANK, LANES), sds(512, LANES), sds(512, LANES), sds(32, LANES)),
                (core, *parts, templates, spectra),
                scalars=1,
            )
            gram = everywhere(gram)
        else:
            templates = call(last_template_body, sds(RANK, PIX), (*parts, templates))
    return state, templates


def solution(mesh):
    grid = Mesh(mesh.devices.reshape(NX, NZ, NC, NY), ("x", "z", "c", "y"))
    every = ("x", "z", "c", "y")
    return jax.shard_map(
        shards,
        mesh=grid,
        in_specs=(P(every, None), P(every, None), P(every), P(every, None), P(None, TGT)),
        out_specs=(P(every, None), P(None, TGT)),
        check_vma=False,
    )
```

```python
import jax
import jax.numpy as jnp
from jax import lax
from jax.experimental import pallas as pl
from jax.experimental.pallas import tpu as pltpu
from jax.sharding import Mesh, PartitionSpec as P

SWEEPS = 2
PRIOR_IVAR = 0.5
EPSILON = 1e-06

NX, NZ, NC, NY = 4, 8, 2, 4
N_TGT = NX * NZ * NC
ROWS = 64
RANK = 64
PIX = 122
LANES = 128
TGT = ("x", "z", "c")
BF = jnp.bfloat16
F32 = jnp.float32
VMEM = pl.BlockSpec(memory_space=pltpu.VMEM)
SMEM = pl.BlockSpec(memory_space=pltpu.SMEM)
NT = (((1,), (1,)), ((), ()))
TN = (((0,), (0,)), ((), ()))


def call(body, outs, args, scratch=(), scalars=0, flops=0):
    return pl.pallas_call(
        body,
        out_shape=outs,
        in_specs=[SMEM] * scalars + [VMEM] * (len(args) - scalars),
        out_specs=jax.tree.map(lambda _: VMEM, outs),
        scratch_shapes=list(scratch),
        compiler_params=pltpu.CompilerParams(vmem_limit_bytes=40 * 2**20),
        cost_estimate=pl.CostEstimate(flops=flops, bytes_accessed=0, transcendentals=0)
        if flops
        else None,
    )(*args)


def pack_body(flux_ref, ivar_ref, target_ref, send_ref, weighted_ref):
    weighted_ref[...] = (
        ivar_ref[...].astype(F32) * flux_ref[...].astype(F32)
    ).astype(BF)
    rows = flux_ref.shape[0]
    at = lax.broadcasted_iota(jnp.int32, (rows, ROWS), 0) + pl.program_id(0) * rows
    here = at == lax.broadcasted_iota(jnp.int32, (rows, ROWS), 1)
    target = jnp.where(here, jnp.broadcast_to(target_ref[...], (rows, ROWS)), 0)
    target = jnp.broadcast_to(jnp.sum(target, axis=1, keepdims=True), (rows, LANES))
    peer, local = target // 128, target % 32
    index = (local // 16) * 1024 + (peer % 2) * 512 + (peer // 2) * 16 + local % 16
    lane = lax.broadcasted_iota(jnp.int32, (rows, LANES), 1)
    extra = jnp.where(lane == 0, index // 64, jnp.where(lane == 1, index % 64, 0))
    extra = extra.astype(F32).astype(BF)
    for dev in range(N_TGT):
        span = slice(dev * PIX, dev * PIX + PIX)
        send_ref[dev, :, 0:PIX] = weighted_ref[:, span]
        send_ref[dev, :, PIX:LANES] = extra[:, 0:LANES - PIX]
        send_ref[dev, :, LANES:LANES + PIX] = ivar_ref[:, span]
        send_ref[dev, :, LANES + PIX:2 * LANES] = jnp.zeros((rows, LANES - PIX), BF)


def pack(flux, ivar, target):
    rows, wide = 32, flux.shape[1]
    return pl.pallas_call(
        pack_body,
        grid=(ROWS // rows,),
        out_shape=sds(N_TGT, ROWS, 2 * LANES, dtype=BF),
        in_specs=[
            pl.BlockSpec((rows, wide), lambda i: (i, 0)),
            pl.BlockSpec((rows, wide), lambda i: (i, 0)),
            pl.BlockSpec((1, ROWS), lambda i: (0, 0)),
        ],
        out_specs=pl.BlockSpec((N_TGT, rows, 2 * LANES), lambda i: (0, i, 0)),
        scratch_shapes=[pltpu.VMEM((rows, wide), BF)],
        compiler_params=pltpu.CompilerParams(vmem_limit_bytes=60 * 2**20),
        cost_estimate=pl.CostEstimate(
            flops=2 * ROWS * wide, bytes_accessed=8 * ROWS * wide, transcendentals=0
        ),
    )(flux, ivar, target)


def template_pair(templ_bf):
    none = jnp.zeros_like(templ_bf)
    return jnp.concatenate(
        [
            jnp.concatenate([templ_bf, none], axis=1),
            jnp.concatenate([none, templ_bf], axis=1),
        ],
        axis=0,
    )


def cross_block(core, block, spectra, pair, keep_ref, send_ref, less=None):
    part = lax.dot_general(spectra, pair, NT, preferred_element_type=F32)
    start = block % 2 * 256
    place = pl.ds(start if isinstance(start, int) else pl.multiple_of(start, 256), 256)

    @pl.when(block // 2 == core)
    def _():
        keep_ref[place, :] = part if less is None else part - less(0, place)

    @pl.when(block // 2 != core)
    def _():
        send_ref[place, :] = part if less is None else part - less(1, place)


def coadd_body(core_ref, got_ref, templ_ref, spectra_ref, keep_ref, send_ref, low_ref, high_ref):
    lane = lax.broadcasted_iota(jnp.int32, (16, 2 * LANES), 1)
    row = lax.broadcasted_iota(jnp.int32, (16, 2 * LANES), 0)
    pick = jnp.where(lane == PIX + row, 1.0, 0.0)
    pick = jnp.where(row < 2, pick, 0.0).astype(BF)
    ids = lax.dot_general(pick, got_ref[...], NT, preferred_element_type=F32)
    high_ref[...] = jnp.broadcast_to(ids[0:1, :], high_ref.shape)
    low = ids[1:2, :].astype(jnp.int32)
    low_ref[...] = jnp.where(
        low == lax.broadcasted_iota(jnp.int32, low_ref.shape, 0), 1.0, 0.0
    ).astype(BF)
    inside = lax.broadcasted_iota(jnp.int32, (256, LANES), 1) < PIX
    pair = template_pair(templ_ref[...].astype(BF))

    def block_step(block, carry):
        first = (block * 4).astype(F32)
        selector = jnp.concatenate(
            [
                low_ref[...]
                * jnp.where(high_ref[0:1, :] == first + float(half * 16 + i), 1.0, 0.0).astype(BF)
                for half in range(2)
                for i in range(4)
            ],
            axis=0,
        )
        sums = jnp.dot(selector, got_ref[...], preferred_element_type=F32)
        coadd = sums[:, 0:LANES] / (sums[:, LANES:] + PRIOR_IVAR)
        for half in range(2):
            spectra_ref[
                pl.ds(pl.multiple_of(block * 256, 256), 256),
                half * LANES:(half + 1) * LANES,
            ] = jnp.where(inside, coadd[half * 256:(half + 1) * 256, :], 0.0).astype(BF)
        spectra = spectra_ref[pl.ds(pl.multiple_of(block * 256, 256), 256), :]
        cross_block(core_ref[0], block, spectra, pair, keep_ref, send_ref)
        return carry

    lax.fori_loop(0, 4, block_step, 0)


def spread(value, lane):
    width = value.shape[1]
    wide = jnp.concatenate(
        [value, jnp.zeros((value.shape[0], LANES - width), F32)], axis=1
    )
    return wide if lane == 0 else pltpu.roll(wide, lane, 1)


def pack_gram(gram):
    top = spread(gram[0:16, :], 0) + spread(gram[16:32, :], 64)
    corner = gram[32:64, 32:64]
    low = sum(spread(corner[8 * i:8 * i + 8, :], 32 * i) for i in range(4))
    return jnp.concatenate([top, low], axis=0)


def unpack_gram(packed):
    top = jnp.concatenate(
        [packed[0:16, :], pltpu.roll(packed[0:16, :], 64, 1)], axis=0
    )[:, 0:RANK]
    low = packed[16:24, :]
    corner = jnp.concatenate(
        [low] + [pltpu.roll(low, LANES - 32 * i, 1) for i in range(1, 4)], axis=0
    )
    side = pad_to(top, LANES, LANES).T[32:64, :]
    lane = lax.broadcasted_iota(jnp.int32, (32, LANES), 1)
    bottom = jnp.where(lane < 32, side, pltpu.roll(corner, 32, 1))
    return jnp.concatenate([top, bottom[:, 0:RANK]], axis=0)


def exact(left, right):
    return jnp.dot(left, right, precision=lax.Precision.HIGHEST, preferred_element_type=F32)


def descend(state, residual, gram):
    eye = lax.broadcasted_iota(jnp.int32, (RANK, RANK), 0) == lax.broadcasted_iota(
        jnp.int32, (RANK, RANK), 1
    )
    pivot = jnp.sum(jnp.where(eye, gram, 0.0), axis=1, keepdims=True) + EPSILON
    inverse = 1.0 / pivot
    goal = state + residual * inverse
    scaled = gram * inverse
    goals = [goal[8 * i:8 * i + 8, :] for i in range(8)]
    done = []
    for k in range(RANK):
        old = state[k:k + 1, :]
        new = jnp.maximum(goals[k // 8][k % 8:k % 8 + 1, :], 0.0)
        done.append(new)
        change = new - old
        for i in range(k // 8, 8):
            goals[i] = goals[i] - scaled[8 * i:8 * i + 8, k:k + 1] * change
    return jnp.concatenate(done, axis=0)


def pad_to(value, rows, lanes):
    if value.shape[1] < lanes:
        value = jnp.concatenate(
            [value, jnp.zeros((value.shape[0], lanes - value.shape[1]), F32)], axis=1
        )
    if value.shape[0] < rows:
        value = jnp.concatenate(
            [value, jnp.zeros((rows - value.shape[0], value.shape[1]), F32)], axis=0
        )
    return value


def activation_body(first, *refs):
    if first:
        cross_ref, gram_ref, state_ref, new_ref, out_ref = refs
    else:
        cross_ref, state_ref, new_ref, out_ref = refs
    total = jnp.sum(cross_ref[...].astype(F32), axis=0)
    cross = pad_to(total[0:16, :], LANES, LANES).T
    wanted = cross[0:64, :] + pltpu.roll(cross[64:128, :], 16, 1)
    gram = unpack_gram(gram_ref[...] if first else total[16:40, :])
    if first:
        state = pad_to(state_ref[...], LANES, LANES).T[0:RANK, :]
    else:
        state = state_ref[...]
    rest = state if first else state - state.astype(BF).astype(F32)
    updated = descend(state, wanted - exact(gram, rest), gram)
    if first:
        new_ref[...] = updated
    else:
        new_ref[...] = pad_to(updated, LANES, LANES).T[0:32, 0:RANK]
    both = jnp.concatenate([updated, pltpu.roll(updated, LANES - 16, 1)], axis=0).T
    out_ref[...] = jnp.broadcast_to(both[0:16, :].astype(BF)[None], out_ref.shape)


def project_body(core_ref, own_ref, other_ref, spectra_ref, out_ref):
    core = core_ref[0]
    proj, gram = 0.0, 0.0
    for ref, at in ((own_ref, core), (other_ref, 1 - core)):
        rows = spectra_ref[pl.ds(pl.multiple_of(at * 512, 512), 512), :]
        proj += lax.dot_general(ref[...], rows, TN, preferred_element_type=F32)
        gram += lax.dot_general(ref[...], ref[...], TN, preferred_element_type=F32)
    out_ref[0:64, :] = proj[0:64, 0:LANES] + proj[64:128, LANES:]
    gram = gram[0:64, 0:64] + pltpu.roll(gram[64:128, :], 64, 1)[:, 0:64]
    out_ref[64:88, :] = pack_gram(gram)


def new_templates(part_refs, templ_ref):
    one, two, three, four = (ref[...] for ref in part_refs)
    total = (one + three) + (two + four)
    templ, gram = templ_ref[...], unpack_gram(total[64:88, :])
    return descend(templ, total[0:64, :] - exact(gram, templ), gram)


def template_body(core_ref, a_ref, b_ref, c_ref, d_ref, templ_ref, own_ref, other_ref, spectra_ref, new_ref, keep_ref, send_ref):
    updated = new_templates((a_ref, b_ref, c_ref, d_ref), templ_ref)
    new_ref[...] = updated
    templ_bf = updated.astype(BF)
    full = lax.dot_general(templ_bf, templ_bf, NT, preferred_element_type=F32)
    square = template_pair(full)
    high = square.astype(BF)
    low = (square - high.astype(F32)).astype(BF)

    def fitted(which, place):
        rows = (own_ref, other_ref)[which][place, :]
        return jnp.dot(rows, high, preferred_element_type=F32) + jnp.dot(
            rows, low, preferred_element_type=F32
        )

    gram = pack_gram(full)
    keep_ref[512:536, :] = gram
    send_ref[512:536, :] = gram
    pair = template_pair(templ_bf)
    for block in range(4):
        spectra = spectra_ref[block * 256:(block + 1) * 256, :]
        cross_block(core_ref[0], block, spectra, pair, keep_ref, send_ref, fitted)


def last_template_body(a_ref, b_ref, c_ref, d_ref, templ_ref, new_ref):
    updated = new_templates((a_ref, b_ref, c_ref, d_ref), templ_ref)
    new_ref[...] = updated[:, 0:PIX]


def first_gram_body(templ_ref, gram_ref):
    templ_bf = templ_ref[...].astype(BF)
    gram_ref[...] = pack_gram(
        lax.dot_general(templ_bf, templ_bf, NT, preferred_element_type=F32)
    )


def shift(value, axis, size, by):
    return lax.ppermute(value, axis, [(i, (i + by) % size) for i in range(size)])


def ring_sum(value, axis, size, step):
    return (value + shift(value, axis, size, 2 * step)) + (
        shift(value, axis, size, step) + shift(value, axis, size, 3 * step)
    )


def from_ahead(value, by):
    pairs = [
        ((z + 2 * y + by) % NZ * NY + y, z * NY + y) for z in range(NZ) for y in range(NY)
    ]
    return lax.ppermute(value, ("z", "y"), pairs)


def two_along_z(part):
    return from_ahead(part, 0) + from_ahead(part, 1)


def near(part):
    return ring_sum(part + shift(part, "c", NC, 1), "x", NX, 1)


def message_body(keep_ref, came_ref, out_ref):
    cross = (keep_ref[0:512, :] + came_ref[0:512, :]).reshape(32, 16, LANES)
    if out_ref.shape[1] > 16:
        gram = keep_ref[512:536, :] + came_ref[512:536, :]
        gram = jnp.broadcast_to(gram[None], (32, 24, LANES))
        cross = jnp.concatenate([cross, gram], axis=1)
    out_ref[...] = cross.astype(out_ref.dtype)


def sds(*shape, dtype=F32):
    return jax.ShapeDtypeStruct(shape, dtype)


def shards(flux, ivar, row_target, start_w, start_h):
    core = lax.axis_index("c").astype(jnp.int32).reshape(1)
    send = pack(flux, ivar, row_target.reshape(1, ROWS))
    templates = jnp.pad(start_h, ((0, 0), (0, LANES - PIX)))
    got = lax.all_to_all(send, TGT, split_axis=0, concat_axis=0, tiled=True)
    gram = near(call(first_gram_body, sds(24, LANES), (templates,)))
    got, gram = lax.optimization_barrier((got, gram))
    gram = two_along_z(gram)
    spectra, keep, away = call(
        coadd_body,
        (sds(1024, 2 * LANES, dtype=BF), sds(512, LANES), sds(512, LANES)),
        (core, got.reshape(N_TGT * ROWS, 2 * LANES), templates),
        scratch=[pltpu.VMEM((64, N_TGT * ROWS), BF), pltpu.VMEM((8, N_TGT * ROWS), F32)],
        scalars=1,
        flops=2 * 2048 * N_TGT * ROWS * 2 * LANES,
    )
    keep, away, gram = lax.optimization_barrier((keep, away, gram))
    gram = ring_sum(gram, "y", NY, 1)
    state = start_w
    for sweep in range(SWEEPS):
        first = sweep == 0
        cross = call(
            message_body,
            sds(32, 16, LANES) if first else sds(32, 40, LANES, dtype=BF),
            (keep, shift(away, "c", NC, 1)),
        )
        cross = lax.all_to_all(cross, ("x", "z"), split_axis=0, concat_axis=0, tiled=True)
        state, message = call(
            lambda *refs, first=first: activation_body(first, *refs),
            (sds(RANK, LANES) if first else sds(32, RANK), sds(32, 16, LANES, dtype=BF)),
            (cross, gram, state) if first else (cross, state),
        )
        own = lax.all_to_all(message, ("x", "z"), split_axis=0, concat_axis=0, tiled=True)
        own = own.reshape(512, LANES)
        other = shift(own, "c", NC, 1)
        part = call(
            project_body, sds(88, LANES), (core, own, other, spectra), scalars=1
        )
        parts = (part, *(shift(part, "y", NY, by) for by in (1, 2, 3)))
        if first:
            templates, keep, away = call(
                template_body,
                (sds(RANK, LANES), sds(536, LANES), sds(536, LANES)),
                (core, *parts, templates, own, other, spectra),
                scalars=1,
            )
        else:
            templates = call(last_template_body, sds(RANK, PIX), (*parts, templates))
    return state, templates


def solution(mesh):
    grid = Mesh(mesh.devices.reshape(NX, NZ, NC, NY), ("x", "z", "c", "y"))
    every = ("x", "z", "c", "y")
    return jax.shard_map(
        shards,
        mesh=grid,
        in_specs=(P(every, None), P(every, None), P(every), P(every, None), P(None, TGT)),
        out_specs=(P(every, None), P(None, TGT)),
        check_vma=False,
    )
```

```python
import jax
import jax.numpy as jnp
from jax import lax
from jax.experimental import pallas as pl
from jax.experimental.pallas import tpu as pltpu
from jax.sharding import Mesh, PartitionSpec as P

SWEEPS = 2
PRIOR_IVAR = 0.5
EPSILON = 1e-06

NX, NZ, NC, NY = 4, 8, 2, 4
N_TGT = NX * NZ * NC
ROWS = 64
RANK = 64
PIX = 122
LANES = 128
TGT = ("x", "z", "c")
BF = jnp.bfloat16
F32 = jnp.float32
VMEM = pl.BlockSpec(memory_space=pltpu.VMEM)
SMEM = pl.BlockSpec(memory_space=pltpu.SMEM)
NT = (((1,), (1,)), ((), ()))
TN = (((0,), (0,)), ((), ()))


def call(body, outs, args, scratch=(), scalars=0, flops=0):
    return pl.pallas_call(
        body,
        out_shape=outs,
        in_specs=[SMEM] * scalars + [VMEM] * (len(args) - scalars),
        out_specs=jax.tree.map(lambda _: VMEM, outs),
        scratch_shapes=list(scratch),
        compiler_params=pltpu.CompilerParams(vmem_limit_bytes=40 * 2**20),
        cost_estimate=pl.CostEstimate(flops=flops, bytes_accessed=0, transcendentals=0)
        if flops
        else None,
    )(*args)


def pack_body(flux_ref, ivar_ref, target_ref, send_ref, weighted_ref):
    weighted_ref[...] = (
        ivar_ref[...].astype(F32) * flux_ref[...].astype(F32)
    ).astype(BF)
    rows = flux_ref.shape[0]
    at = lax.broadcasted_iota(jnp.int32, (rows, ROWS), 0) + pl.program_id(0) * rows
    here = at == lax.broadcasted_iota(jnp.int32, (rows, ROWS), 1)
    target = jnp.where(here, jnp.broadcast_to(target_ref[...], (rows, ROWS)), 0)
    target = jnp.broadcast_to(jnp.sum(target, axis=1, keepdims=True), (rows, LANES))
    peer, local = target // 128, target % 32
    index = (local // 16) * 1024 + (peer % 2) * 512 + (peer // 2) * 16 + local % 16
    lane = lax.broadcasted_iota(jnp.int32, (rows, LANES), 1)
    extra = jnp.where(lane == 0, index // 64, jnp.where(lane == 1, index % 64, 0))
    extra = extra.astype(F32).astype(BF)
    for dev in range(N_TGT):
        span = slice(dev * PIX, dev * PIX + PIX)
        send_ref[dev, :, 0:PIX] = weighted_ref[:, span]
        send_ref[dev, :, PIX:LANES] = extra[:, 0:LANES - PIX]
        send_ref[dev, :, LANES:LANES + PIX] = ivar_ref[:, span]
        send_ref[dev, :, LANES + PIX:2 * LANES] = jnp.zeros((rows, LANES - PIX), BF)


def pack(flux, ivar, target):
    rows, wide = 32, flux.shape[1]
    return pl.pallas_call(
        pack_body,
        grid=(ROWS // rows,),
        out_shape=sds(N_TGT, ROWS, 2 * LANES, dtype=BF),
        in_specs=[
            pl.BlockSpec((rows, wide), lambda i: (i, 0)),
            pl.BlockSpec((rows, wide), lambda i: (i, 0)),
            pl.BlockSpec((1, ROWS), lambda i: (0, 0)),
        ],
        out_specs=pl.BlockSpec((N_TGT, rows, 2 * LANES), lambda i: (0, i, 0)),
        scratch_shapes=[pltpu.VMEM((rows, wide), BF)],
        compiler_params=pltpu.CompilerParams(vmem_limit_bytes=60 * 2**20),
        cost_estimate=pl.CostEstimate(
            flops=2 * ROWS * wide, bytes_accessed=8 * ROWS * wide, transcendentals=0
        ),
    )(flux, ivar, target)


def template_pair(templ_bf):
    none = jnp.zeros_like(templ_bf)
    return jnp.concatenate(
        [
            jnp.concatenate([templ_bf, none], axis=1),
            jnp.concatenate([none, templ_bf], axis=1),
        ],
        axis=0,
    )


def cross_block(core, block, spectra, pair, keep_ref, send_ref, less=None):
    part = lax.dot_general(spectra, pair, NT, preferred_element_type=F32)
    start = block % 2 * 256
    place = pl.ds(start if isinstance(start, int) else pl.multiple_of(start, 256), 256)

    @pl.when(block // 2 == core)
    def _():
        keep_ref[place, :] = part if less is None else part - less(0, place)

    @pl.when(block // 2 != core)
    def _():
        send_ref[place, :] = part if less is None else part - less(1, place)


def coadd_body(core_ref, got_ref, templ_ref, spectra_ref, keep_ref, send_ref, low_ref, high_ref):
    lane = lax.broadcasted_iota(jnp.int32, (16, 2 * LANES), 1)
    row = lax.broadcasted_iota(jnp.int32, (16, 2 * LANES), 0)
    pick = jnp.where(lane == PIX + row, 1.0, 0.0)
    pick = jnp.where(row < 2, pick, 0.0).astype(BF)
    ids = lax.dot_general(pick, got_ref[...], NT, preferred_element_type=F32)
    high_ref[...] = jnp.broadcast_to(ids[0:1, :], high_ref.shape)
    low = ids[1:2, :].astype(jnp.int32)
    low_ref[...] = jnp.where(
        low == lax.broadcasted_iota(jnp.int32, low_ref.shape, 0), 1.0, 0.0
    ).astype(BF)
    inside = lax.broadcasted_iota(jnp.int32, (256, LANES), 1) < PIX
    pair = template_pair(templ_ref[...].astype(BF))

    def block_step(block, carry):
        first = (block * 4).astype(F32)
        selector = jnp.concatenate(
            [
                low_ref[...]
                * jnp.where(high_ref[0:1, :] == first + float(half * 16 + i), 1.0, 0.0).astype(BF)
                for half in range(2)
                for i in range(4)
            ],
            axis=0,
        )
        sums = jnp.dot(selector, got_ref[...], preferred_element_type=F32)
        coadd = sums[:, 0:LANES] / (sums[:, LANES:] + PRIOR_IVAR)
        for half in range(2):
            spectra_ref[
                pl.ds(pl.multiple_of(block * 256, 256), 256),
                half * LANES:(half + 1) * LANES,
            ] = jnp.where(inside, coadd[half * 256:(half + 1) * 256, :], 0.0).astype(BF)
        spectra = spectra_ref[pl.ds(pl.multiple_of(block * 256, 256), 256), :]
        cross_block(core_ref[0], block, spectra, pair, keep_ref, send_ref)
        return carry

    lax.fori_loop(0, 4, block_step, 0)


def spread(value, lane):
    width = value.shape[1]
    wide = jnp.concatenate(
        [value, jnp.zeros((value.shape[0], LANES - width), F32)], axis=1
    )
    return wide if lane == 0 else pltpu.roll(wide, lane, 1)


def pack_gram(gram):
    top = spread(gram[0:16, :], 0) + spread(gram[16:32, :], 64)
    corner = gram[32:64, 32:64]
    low = sum(spread(corner[8 * i:8 * i + 8, :], 32 * i) for i in range(4))
    return jnp.concatenate([top, low], axis=0)


def unpack_gram(packed):
    top = jnp.concatenate(
        [packed[0:16, :], pltpu.roll(packed[0:16, :], 64, 1)], axis=0
    )[:, 0:RANK]
    low = packed[16:24, :]
    corner = jnp.concatenate(
        [low] + [pltpu.roll(low, LANES - 32 * i, 1) for i in range(1, 4)], axis=0
    )
    side = pad_to(top, LANES, LANES).T[32:64, :]
    lane = lax.broadcasted_iota(jnp.int32, (32, LANES), 1)
    bottom = jnp.where(lane < 32, side, pltpu.roll(corner, 32, 1))
    return jnp.concatenate([top, bottom[:, 0:RANK]], axis=0)


def exact(left, right):
    return jnp.dot(left, right, precision=lax.Precision.HIGHEST, preferred_element_type=F32)


def descend(state, residual, gram):
    eye = lax.broadcasted_iota(jnp.int32, (RANK, RANK), 0) == lax.broadcasted_iota(
        jnp.int32, (RANK, RANK), 1
    )
    pivot = jnp.sum(jnp.where(eye, gram, 0.0), axis=1, keepdims=True) + EPSILON
    inverse = 1.0 / pivot
    goal = state + residual * inverse
    scaled = gram * inverse
    goals = [goal[8 * i:8 * i + 8, :] for i in range(8)]
    done = []
    for k in range(RANK):
        old = state[k:k + 1, :]
        new = jnp.maximum(goals[k // 8][k % 8:k % 8 + 1, :], 0.0)
        done.append(new)
        change = new - old
        for i in range(k // 8, 8):
            goals[i] = goals[i] - scaled[8 * i:8 * i + 8, k:k + 1] * change
    return jnp.concatenate(done, axis=0)


def pad_to(value, rows, lanes):
    if value.shape[1] < lanes:
        value = jnp.concatenate(
            [value, jnp.zeros((value.shape[0], lanes - value.shape[1]), F32)], axis=1
        )
    if value.shape[0] < rows:
        value = jnp.concatenate(
            [value, jnp.zeros((rows - value.shape[0], value.shape[1]), F32)], axis=0
        )
    return value


def activation_body(first, *refs):
    cross_ref, state_ref, new_ref, out_ref = refs
    total = jnp.sum(cross_ref[...].astype(F32), axis=0)
    cross = pad_to(total[0:16, :], LANES, LANES).T
    wanted = cross[0:64, :] + pltpu.roll(cross[64:128, :], 16, 1)
    if first:
        packed = jnp.concatenate(
            [jnp.sum(cross_ref[NZ * i:NZ * i + NZ, 16:24, :], axis=0) for i in range(NX)],
            axis=0,
        )
        gram = jnp.concatenate(
            [packed[:, 0:RANK], pltpu.roll(packed, RANK, 1)[:, 0:RANK]], axis=0
        )
    else:
        gram = unpack_gram(total[16:40, :])
    if first:
        state = pad_to(state_ref[...], LANES, LANES).T[0:RANK, :]
    else:
        state = state_ref[...]
    rest = state if first else state - state.astype(BF).astype(F32)
    updated = descend(state, wanted - exact(gram, rest), gram)
    if first:
        new_ref[...] = updated
    else:
        new_ref[...] = pad_to(updated, LANES, LANES).T[0:32, 0:RANK]
    both = jnp.concatenate([updated, pltpu.roll(updated, LANES - 16, 1)], axis=0).T
    out_ref[...] = jnp.broadcast_to(both[0:16, :].astype(BF)[None], out_ref.shape)


def project_body(core_ref, own_ref, other_ref, spectra_ref, out_ref):
    core = core_ref[0]
    proj, gram = 0.0, 0.0
    for ref, at in ((own_ref, core), (other_ref, 1 - core)):
        rows = spectra_ref[pl.ds(pl.multiple_of(at * 512, 512), 512), :]
        proj += lax.dot_general(ref[...], rows, TN, preferred_element_type=F32)
        gram += lax.dot_general(ref[...], ref[...], TN, preferred_element_type=F32)
    out_ref[0:64, :] = proj[0:64, 0:LANES] + proj[64:128, LANES:]
    gram = gram[0:64, 0:64] + pltpu.roll(gram[64:128, :], 64, 1)[:, 0:64]
    out_ref[64:88, :] = pack_gram(gram)


def new_templates(part_refs, templ_ref):
    total = part_refs[0][...] + part_refs[1][...]
    templ, gram = templ_ref[...], unpack_gram(total[64:88, :])
    return descend(templ, total[0:64, :] - exact(gram, templ), gram)


def template_body(core_ref, a_ref, b_ref, templ_ref, own_ref, other_ref, spectra_ref, new_ref, keep_ref, send_ref):
    updated = new_templates((a_ref, b_ref), templ_ref)
    new_ref[...] = updated
    templ_bf = updated.astype(BF)
    full = lax.dot_general(templ_bf, templ_bf, NT, preferred_element_type=F32)
    square = template_pair(full)
    high = square.astype(BF)
    low = (square - high.astype(F32)).astype(BF)

    def fitted(which, place):
        rows = (own_ref, other_ref)[which][place, :]
        return jnp.dot(rows, high, preferred_element_type=F32) + jnp.dot(
            rows, low, preferred_element_type=F32
        )

    gram = pack_gram(full)
    keep_ref[512:536, :] = gram
    send_ref[512:536, :] = gram
    pair = template_pair(templ_bf)
    for block in range(4):
        spectra = spectra_ref[block * 256:(block + 1) * 256, :]
        cross_block(core_ref[0], block, spectra, pair, keep_ref, send_ref, fitted)


def last_template_body(a_ref, b_ref, templ_ref, new_ref):
    updated = new_templates((a_ref, b_ref), templ_ref)
    new_ref[...] = updated[:, 0:PIX]


def first_gram_body(templ_ref, gram_ref):
    templ_bf = templ_ref[...].astype(BF)
    gram = lax.dot_general(templ_bf, templ_bf, NT, preferred_element_type=F32)
    gram_ref[...] = spread(gram[0:32, :], 0) + spread(gram[32:64, :], 64)


def shift(value, axis, size, by):
    return lax.ppermute(value, axis, [(i, (i + by) % size) for i in range(size)])


def ring_sum(value, axis, size, step):
    return (value + shift(value, axis, size, 2 * step)) + (
        shift(value, axis, size, step) + shift(value, axis, size, 3 * step)
    )


def near(part):
    return ring_sum(part + shift(part, "c", NC, 1), "x", NX, 1)


def first_message_body(quarter_ref, gram_ref, keep_ref, came_ref, out_ref):
    rows = pl.ds(pl.multiple_of(quarter_ref[0] * 8, 8), 8)
    out_ref[:, 0:16, :] = (keep_ref[...] + came_ref[...]).reshape(32, 16, LANES)
    out_ref[:, 16:24, :] = jnp.broadcast_to(gram_ref[rows, :][None], (32, 8, LANES))


def message_body(keep_ref, came_ref, out_ref):
    cross = (keep_ref[0:512, :] + came_ref[0:512, :]).reshape(32, 16, LANES)
    gram = keep_ref[512:536, :] + came_ref[512:536, :]
    gram = jnp.broadcast_to(gram[None], (32, 24, LANES))
    out_ref[...] = jnp.concatenate([cross, gram], axis=1).astype(BF)


def sds(*shape, dtype=F32):
    return jax.ShapeDtypeStruct(shape, dtype)


def shards(flux, ivar, row_target, start_w, start_h):
    core = lax.axis_index("c").astype(jnp.int32).reshape(1)
    send = pack(flux, ivar, row_target.reshape(1, ROWS))
    templates = jnp.pad(start_h, ((0, 0), (0, LANES - PIX)))
    got = lax.all_to_all(send, TGT, split_axis=0, concat_axis=0, tiled=True)
    gram = near(call(first_gram_body, sds(32, LANES), (templates,)))
    got, gram = lax.optimization_barrier((got, gram))
    spectra, keep, away = call(
        coadd_body,
        (sds(1024, 2 * LANES, dtype=BF), sds(512, LANES), sds(512, LANES)),
        (core, got.reshape(N_TGT * ROWS, 2 * LANES), templates),
        scratch=[pltpu.VMEM((64, N_TGT * ROWS), BF), pltpu.VMEM((8, N_TGT * ROWS), F32)],
        scalars=1,
        flops=2 * 2048 * N_TGT * ROWS * 2 * LANES,
    )
    state = start_w
    for sweep in range(SWEEPS):
        first = sweep == 0
        came = shift(away, "c", NC, 1)
        if first:
            cross = call(
                first_message_body,
                sds(32, 24, LANES),
                (lax.axis_index("x").astype(jnp.int32).reshape(1), gram, keep, came),
                scalars=1,
            )
        else:
            cross = call(message_body, sds(32, 40, LANES, dtype=BF), (keep, came))
        cross = lax.all_to_all(cross, ("x", "z"), split_axis=0, concat_axis=0, tiled=True)
        state, message = call(
            lambda *refs, first=first: activation_body(first, *refs),
            (sds(RANK, LANES) if first else sds(32, RANK), sds(32, 16, LANES, dtype=BF)),
            (cross, state),
        )
        own = lax.all_to_all(message, ("x", "z"), split_axis=0, concat_axis=0, tiled=True)
        own = own.reshape(512, LANES)
        other = shift(own, "c", NC, 1)
        part = call(
            project_body, sds(88, LANES), (core, own, other, spectra), scalars=1
        )
        part = part + lax.ppermute(part, "y", [(0, 1), (1, 0), (2, 3), (3, 2)])
        parts = (part, lax.ppermute(part, "y", [(0, 3), (3, 0), (1, 2), (2, 1)]))
        if first:
            templates, keep, away = call(
                template_body,
                (sds(RANK, LANES), sds(536, LANES), sds(536, LANES)),
                (core, *parts, templates, own, other, spectra),
                scalars=1,
            )
        else:
            templates = call(last_template_body, sds(RANK, PIX), (*parts, templates))
    return state, templates


def solution(mesh):
    grid = Mesh(mesh.devices.reshape(NX, NZ, NC, NY), ("x", "z", "c", "y"))
    every = ("x", "z", "c", "y")
    return jax.shard_map(
        shards,
        mesh=grid,
        in_specs=(P(every, None), P(every, None), P(every), P(every, None), P(None, TGT)),
        out_specs=(P(every, None), P(None, TGT)),
        check_vma=False,
    )
```

```python
import jax
import jax.numpy as jnp
from jax import lax
from jax.experimental import pallas as pl
from jax.experimental.pallas import tpu as pltpu
from jax.sharding import Mesh, PartitionSpec as P

SWEEPS = 2
PRIOR_IVAR = 0.5
EPSILON = 1e-06

NX, NZ, NC, NY = 4, 8, 2, 4
N_TGT = NX * NZ * NC
ROWS = 64
RANK = 64
PIX = 122
LANES = 128
TGT = ("x", "z", "c")
BF = jnp.bfloat16
F32 = jnp.float32
VMEM = pl.BlockSpec(memory_space=pltpu.VMEM)
SMEM = pl.BlockSpec(memory_space=pltpu.SMEM)
NT = (((1,), (1,)), ((), ()))
TN = (((0,), (0,)), ((), ()))


def call(body, outs, args, scratch=(), scalars=0, flops=0):
    return pl.pallas_call(
        body,
        out_shape=outs,
        in_specs=[SMEM] * scalars + [VMEM] * (len(args) - scalars),
        out_specs=jax.tree.map(lambda _: VMEM, outs),
        scratch_shapes=list(scratch),
        compiler_params=pltpu.CompilerParams(vmem_limit_bytes=40 * 2**20),
        cost_estimate=pl.CostEstimate(flops=flops, bytes_accessed=0, transcendentals=0)
        if flops
        else None,
    )(*args)


def pack_body(flux_ref, ivar_ref, target_ref, send_ref, weighted_ref):
    weighted_ref[...] = (
        ivar_ref[...].astype(F32) * flux_ref[...].astype(F32)
    ).astype(BF)
    rows = flux_ref.shape[0]
    at = lax.broadcasted_iota(jnp.int32, (rows, ROWS), 0) + pl.program_id(0) * rows
    here = at == lax.broadcasted_iota(jnp.int32, (rows, ROWS), 1)
    target = jnp.where(here, jnp.broadcast_to(target_ref[...], (rows, ROWS)), 0)
    target = jnp.broadcast_to(jnp.sum(target, axis=1, keepdims=True), (rows, LANES))
    peer, local = target // 128, target % 32
    index = (local // 16) * 1024 + (peer % 2) * 512 + (peer // 2) * 16 + local % 16
    lane = lax.broadcasted_iota(jnp.int32, (rows, LANES), 1)
    extra = jnp.where(lane == 0, index // 64, jnp.where(lane == 1, index % 64, 0))
    extra = extra.astype(F32).astype(BF)
    for dev in range(N_TGT):
        span = slice(dev * PIX, dev * PIX + PIX)
        send_ref[dev, :, 0:PIX] = weighted_ref[:, span]
        send_ref[dev, :, PIX:LANES] = extra[:, 0:LANES - PIX]
        send_ref[dev, :, LANES:LANES + PIX] = ivar_ref[:, span]
        send_ref[dev, :, LANES + PIX:2 * LANES] = jnp.zeros((rows, LANES - PIX), BF)


def pack(flux, ivar, target):
    rows, wide = 32, flux.shape[1]
    return pl.pallas_call(
        pack_body,
        grid=(ROWS // rows,),
        out_shape=sds(N_TGT, ROWS, 2 * LANES, dtype=BF),
        in_specs=[
            pl.BlockSpec((rows, wide), lambda i: (i, 0)),
            pl.BlockSpec((rows, wide), lambda i: (i, 0)),
            pl.BlockSpec((1, ROWS), lambda i: (0, 0)),
        ],
        out_specs=pl.BlockSpec((N_TGT, rows, 2 * LANES), lambda i: (0, i, 0)),
        scratch_shapes=[pltpu.VMEM((rows, wide), BF)],
        compiler_params=pltpu.CompilerParams(vmem_limit_bytes=60 * 2**20),
        cost_estimate=pl.CostEstimate(
            flops=2 * ROWS * wide, bytes_accessed=8 * ROWS * wide, transcendentals=0
        ),
    )(flux, ivar, target)


def template_pair(templ_bf):
    none = jnp.zeros_like(templ_bf)
    return jnp.concatenate(
        [
            jnp.concatenate([templ_bf, none], axis=1),
            jnp.concatenate([none, templ_bf], axis=1),
        ],
        axis=0,
    )


def coadd_rows(core, got_ref, low_ref, high_ref, spectra_ref):
    inside = lax.broadcasted_iota(jnp.int32, (256, LANES), 1) < PIX

    def block_step(block, carry):
        first = (core * 8 + block * 4).astype(F32)
        selector = jnp.concatenate(
            [
                low_ref[...]
                * jnp.where(high_ref[0:1, :] == first + float(half * 16 + i), 1.0, 0.0).astype(BF)
                for half in range(2)
                for i in range(4)
            ],
            axis=0,
        )
        sums = jnp.dot(selector, got_ref[...], preferred_element_type=F32)
        coadd = sums[:, 0:LANES] / (sums[:, LANES:] + PRIOR_IVAR)
        for half in range(2):
            spectra_ref[
                pl.ds(pl.multiple_of(block * 256, 256), 256),
                half * LANES:(half + 1) * LANES,
            ] = jnp.where(inside, coadd[half * 256:(half + 1) * 256, :], 0.0).astype(BF)
        return carry

    lax.fori_loop(0, 2, block_step, 0)


def away_body(core_ref, got_ref, away_ref, low_ref, high_ref):
    lane = lax.broadcasted_iota(jnp.int32, (16, 2 * LANES), 1)
    row = lax.broadcasted_iota(jnp.int32, (16, 2 * LANES), 0)
    pick = jnp.where(lane == PIX + row, 1.0, 0.0)
    pick = jnp.where(row < 2, pick, 0.0).astype(BF)
    ids = lax.dot_general(pick, got_ref[...], NT, preferred_element_type=F32)
    high_ref[...] = jnp.broadcast_to(ids[0:1, :], high_ref.shape)
    low = ids[1:2, :].astype(jnp.int32)
    low_ref[...] = jnp.where(
        low == lax.broadcasted_iota(jnp.int32, low_ref.shape, 0), 1.0, 0.0
    ).astype(BF)
    coadd_rows(1 - core_ref[0], got_ref, low_ref, high_ref, away_ref)


def keep_body(core_ref, got_ref, low_ref, high_ref, keep_ref):
    coadd_rows(core_ref[0], got_ref, low_ref, high_ref, keep_ref)


def cross_of(keep_ref, came_ref, own_bf, other_bf):
    return lax.dot_general(
        keep_ref[...], template_pair(own_bf), NT, preferred_element_type=F32
    ) + lax.dot_general(
        came_ref[...], template_pair(other_bf), NT, preferred_element_type=F32
    )


def spread(value, lane):
    width = value.shape[1]
    wide = jnp.concatenate(
        [value, jnp.zeros((value.shape[0], LANES - width), F32)], axis=1
    )
    return wide if lane == 0 else pltpu.roll(wide, lane, 1)


def pack_gram(gram):
    top = spread(gram[0:16, :], 0) + spread(gram[16:32, :], 64)
    corner = gram[32:64, 32:64]
    low = sum(spread(corner[8 * i:8 * i + 8, :], 32 * i) for i in range(4))
    return jnp.concatenate([top, low], axis=0)


def unpack_gram(packed):
    top = jnp.concatenate(
        [packed[0:16, :], pltpu.roll(packed[0:16, :], 64, 1)], axis=0
    )[:, 0:RANK]
    low = packed[16:24, :]
    corner = jnp.concatenate(
        [low] + [pltpu.roll(low, LANES - 32 * i, 1) for i in range(1, 4)], axis=0
    )
    side = pad_to(top, LANES, LANES).T[32:64, :]
    lane = lax.broadcasted_iota(jnp.int32, (32, LANES), 1)
    bottom = jnp.where(lane < 32, side, pltpu.roll(corner, 32, 1))
    return jnp.concatenate([top, bottom[:, 0:RANK]], axis=0)


def exact(left, right):
    return jnp.dot(left, right, precision=lax.Precision.HIGHEST, preferred_element_type=F32)


def descend(state, residual, gram):
    eye = lax.broadcasted_iota(jnp.int32, (RANK, RANK), 0) == lax.broadcasted_iota(
        jnp.int32, (RANK, RANK), 1
    )
    pivot = jnp.sum(jnp.where(eye, gram, 0.0), axis=1, keepdims=True) + EPSILON
    inverse = 1.0 / pivot
    goal = state + residual * inverse
    scaled = gram * inverse
    goals = [goal[8 * i:8 * i + 8, :] for i in range(8)]
    done = []
    for k in range(RANK):
        old = state[k:k + 1, :]
        new = jnp.maximum(goals[k // 8][k % 8:k % 8 + 1, :], 0.0)
        done.append(new)
        change = new - old
        for i in range(k // 8, 8):
            goals[i] = goals[i] - scaled[8 * i:8 * i + 8, k:k + 1] * change
    return jnp.concatenate(done, axis=0)


def pad_to(value, rows, lanes):
    if value.shape[1] < lanes:
        value = jnp.concatenate(
            [value, jnp.zeros((value.shape[0], lanes - value.shape[1]), F32)], axis=1
        )
    if value.shape[0] < rows:
        value = jnp.concatenate(
            [value, jnp.zeros((rows - value.shape[0], value.shape[1]), F32)], axis=0
        )
    return value


def activation_body(first, *refs):
    cross_ref, state_ref, new_ref, out_ref = refs
    total = jnp.sum(cross_ref[...].astype(F32), axis=0)
    cross = pad_to(total[0:16, :], LANES, LANES).T
    wanted = cross[0:64, :] + pltpu.roll(cross[64:128, :], 16, 1)
    if first:
        packed = jnp.concatenate(
            [jnp.sum(cross_ref[NZ * i:NZ * i + NZ, 16:24, :], axis=0) for i in range(NX)],
            axis=0,
        )
        gram = jnp.concatenate(
            [packed[:, 0:RANK], pltpu.roll(packed, RANK, 1)[:, 0:RANK]], axis=0
        )
    else:
        gram = unpack_gram(total[16:40, :])
    if first:
        state = pad_to(state_ref[...], LANES, LANES).T[0:RANK, :]
    else:
        state = state_ref[...]
    rest = state if first else state - state.astype(BF).astype(F32)
    updated = descend(state, wanted - exact(gram, rest), gram)
    if first:
        new_ref[...] = updated
    else:
        new_ref[...] = pad_to(updated, LANES, LANES).T[0:32, 0:RANK]
    both = jnp.concatenate([updated, pltpu.roll(updated, LANES - 16, 1)], axis=0).T
    out_ref[...] = jnp.broadcast_to(both[0:16, :].astype(BF)[None], out_ref.shape)


def project_body(activ_ref, keep_ref, came_ref, own_ref, send_ref):
    activ = activ_ref[...]
    gram = lax.dot_general(activ, activ, TN, preferred_element_type=F32)
    gram = pack_gram(gram[0:64, 0:64] + pltpu.roll(gram[64:128, :], 64, 1)[:, 0:64])
    blocks = []
    for ref in (keep_ref, came_ref):
        proj = lax.dot_general(activ, ref[...], TN, preferred_element_type=F32)
        blocks.append(proj[0:64, 0:LANES] + proj[64:128, LANES:])
    own_ref[0:24, :] = gram
    own_ref[24:88, :] = blocks[0]
    send_ref[0:24, :] = gram
    send_ref[24:88, :] = blocks[1]
    if own_ref.shape[0] > 88:
        own_ref[88:152, :] = blocks[1]
        send_ref[24:88, :] = blocks[1]
        send_ref[88:152, :] = blocks[0]


def new_templates(part_refs, templ):
    one, two, three, four = (ref[...] for ref in part_refs)
    total = (one + three) + (two + four)
    gram, proj = unpack_gram(total[0:24, :]), total[24:88, :]
    if total.shape[0] > 88:
        proj = jnp.concatenate([proj, total[88:152, :]], axis=1)
    return descend(templ, proj - exact(gram, templ), gram)


def template_body(a_ref, b_ref, c_ref, d_ref, own_ref, other_ref, activ_ref, keep_ref, came_ref, new_ref, out_ref):
    templ = jnp.concatenate([own_ref[...], other_ref[...]], axis=1)
    updated = new_templates((a_ref, b_ref, c_ref, d_ref), templ)
    new_ref[...] = updated[:, 0:LANES]
    templ_bf = updated.astype(BF)
    full = lax.dot_general(templ_bf, templ_bf, NT, preferred_element_type=F32)
    square = template_pair(full)
    high = square.astype(BF)
    low = (square - high.astype(F32)).astype(BF)
    rows = activ_ref[...]
    fitted = jnp.dot(rows, high, preferred_element_type=F32) + jnp.dot(
        rows, low, preferred_element_type=F32
    )
    cross = cross_of(keep_ref, came_ref, templ_bf[:, 0:LANES], templ_bf[:, LANES:]) - fitted
    gram = jnp.broadcast_to(pack_gram(full)[None], (32, 24, LANES))
    out_ref[...] = jnp.concatenate([cross.reshape(32, 16, LANES), gram], axis=1).astype(BF)


def last_template_body(a_ref, b_ref, c_ref, d_ref, templ_ref, new_ref):
    updated = new_templates((a_ref, b_ref, c_ref, d_ref), templ_ref[...])
    new_ref[...] = updated[:, 0:PIX]


def first_gram_body(templ_ref, gram_ref):
    templ_bf = templ_ref[...].astype(BF)
    gram = lax.dot_general(templ_bf, templ_bf, NT, preferred_element_type=F32)
    gram_ref[...] = spread(gram[0:32, :], 0) + spread(gram[32:64, :], 64)


def shift(value, axis, size, by):
    return lax.ppermute(value, axis, [(i, (i + by) % size) for i in range(size)])


def ring_sum(value, axis, size, step):
    return (value + shift(value, axis, size, 2 * step)) + (
        shift(value, axis, size, step) + shift(value, axis, size, 3 * step)
    )


def near(part):
    return ring_sum(part + shift(part, "c", NC, 1), "x", NX, 1)


def first_message_body(quarter_ref, gram_ref, own_ref, other_ref, keep_ref, came_ref, out_ref):
    rows = pl.ds(pl.multiple_of(quarter_ref[0] * 8, 8), 8)
    cross = cross_of(keep_ref, came_ref, own_ref[...].astype(BF), other_ref[...].astype(BF))
    out_ref[:, 0:16, :] = cross.reshape(32, 16, LANES)
    out_ref[:, 16:24, :] = jnp.broadcast_to(gram_ref[rows, :][None], (32, 8, LANES))


def sds(*shape, dtype=F32):
    return jax.ShapeDtypeStruct(shape, dtype)


def shards(flux, ivar, row_target, start_w, start_h):
    core = lax.axis_index("c").astype(jnp.int32).reshape(1)
    send = pack(flux, ivar, row_target.reshape(1, ROWS))
    templates = jnp.pad(start_h, ((0, 0), (0, LANES - PIX)))
    got = lax.all_to_all(send, TGT, split_axis=0, concat_axis=0, tiled=True)
    gram = near(call(first_gram_body, sds(32, LANES), (templates,)))
    other = shift(templates, "c", NC, 1)
    got, gram, other = lax.optimization_barrier((got, gram, other))
    rows = got.reshape(N_TGT * ROWS, 2 * LANES)
    half = sds(512, 2 * LANES, dtype=BF)
    cost = 2 * 1024 * N_TGT * ROWS * 2 * LANES
    away, low, high = call(
        away_body,
        (half, sds(64, N_TGT * ROWS, dtype=BF), sds(8, N_TGT * ROWS)),
        (core, rows),
        scalars=1,
        flops=cost,
    )
    came = shift(away, "c", NC, 1)
    keep = call(keep_body, half, (core, rows, low, high), scalars=1, flops=cost)
    quarter = lax.axis_index("x").astype(jnp.int32).reshape(1)
    cross = call(
        first_message_body,
        sds(32, 24, LANES),
        (quarter, gram, templates, other, keep, came),
        scalars=1,
    )
    state = start_w
    for sweep in range(SWEEPS):
        first = sweep == 0
        cross = lax.all_to_all(cross, ("x", "z"), split_axis=0, concat_axis=0, tiled=True)
        state, message = call(
            lambda *refs, first=first: activation_body(first, *refs),
            (sds(RANK, LANES) if first else sds(32, RANK), sds(32, 16, LANES, dtype=BF)),
            (cross, state),
        )
        activ = lax.all_to_all(message, ("x", "z"), split_axis=0, concat_axis=0, tiled=True)
        activ = activ.reshape(512, LANES)
        size = 152 if first else 88
        part, away = call(
            project_body, (sds(size, LANES), sds(size, LANES)), (activ, keep, came)
        )
        part = part + shift(away, "c", NC, 1)
        parts = (part, *(shift(part, "y", NY, by) for by in (1, 2, 3)))
        if first:
            templates, cross = call(
                template_body,
                (sds(RANK, LANES), sds(32, 40, LANES, dtype=BF)),
                (*parts, templates, other, activ, keep, came),
            )
        else:
            templates = call(last_template_body, sds(RANK, PIX), (*parts, templates))
    return state, templates


def solution(mesh):
    grid = Mesh(mesh.devices.reshape(NX, NZ, NC, NY), ("x", "z", "c", "y"))
    every = ("x", "z", "c", "y")
    return jax.shard_map(
        shards,
        mesh=grid,
        in_specs=(P(every, None), P(every, None), P(every), P(every, None), P(None, TGT)),
        out_specs=(P(every, None), P(None, TGT)),
        check_vma=False,
    )
```

```python
import jax
import jax.numpy as jnp
from jax import lax
from jax.experimental import pallas as pl
from jax.experimental.pallas import tpu as pltpu
from jax.sharding import Mesh, PartitionSpec as P

SWEEPS = 2
PRIOR_IVAR = 0.5
EPSILON = 1e-06

NX, NZ, NC, NY = 4, 8, 2, 4
N_TGT = NX * NZ * NC
ROWS = 64
RANK = 64
PIX = 122
LANES = 128
TGT = ("x", "z", "c")
BF = jnp.bfloat16
F32 = jnp.float32
VMEM = pl.BlockSpec(memory_space=pltpu.VMEM)
SMEM = pl.BlockSpec(memory_space=pltpu.SMEM)
NT = (((1,), (1,)), ((), ()))
TN = (((0,), (0,)), ((), ()))


def call(body, outs, args, scratch=(), scalars=0, flops=0):
    return pl.pallas_call(
        body,
        out_shape=outs,
        in_specs=[SMEM] * scalars + [VMEM] * (len(args) - scalars),
        out_specs=jax.tree.map(lambda _: VMEM, outs),
        scratch_shapes=list(scratch),
        compiler_params=pltpu.CompilerParams(vmem_limit_bytes=40 * 2**20),
        cost_estimate=pl.CostEstimate(flops=flops, bytes_accessed=0, transcendentals=0)
        if flops
        else None,
    )(*args)


def pack_body(flux_ref, ivar_ref, target_ref, send_ref, weighted_ref):
    weighted_ref[...] = (
        ivar_ref[...].astype(F32) * flux_ref[...].astype(F32)
    ).astype(BF)
    rows = flux_ref.shape[0]
    at = lax.broadcasted_iota(jnp.int32, (rows, ROWS), 0) + pl.program_id(0) * rows
    here = at == lax.broadcasted_iota(jnp.int32, (rows, ROWS), 1)
    target = jnp.where(here, jnp.broadcast_to(target_ref[...], (rows, ROWS)), 0)
    target = jnp.broadcast_to(jnp.sum(target, axis=1, keepdims=True), (rows, LANES))
    peer, local = target // 128, target % 32
    index = (local // 16) * 1024 + (peer % 2) * 512 + (peer // 2) * 16 + local % 16
    lane = lax.broadcasted_iota(jnp.int32, (rows, LANES), 1)
    extra = jnp.where(lane == 0, index // 64, jnp.where(lane == 1, index % 64, 0))
    extra = extra.astype(F32).astype(BF)
    for dev in range(N_TGT):
        span = slice(dev * PIX, dev * PIX + PIX)
        send_ref[dev, :, 0:PIX] = weighted_ref[:, span]
        send_ref[dev, :, PIX:LANES] = extra[:, 0:LANES - PIX]
        send_ref[dev, :, LANES:LANES + PIX] = ivar_ref[:, span]
        send_ref[dev, :, LANES + PIX:2 * LANES] = jnp.zeros((rows, LANES - PIX), BF)


def pack(flux, ivar, target):
    rows, wide = 32, flux.shape[1]
    return pl.pallas_call(
        pack_body,
        grid=(ROWS // rows,),
        out_shape=sds(N_TGT, ROWS, 2 * LANES, dtype=BF),
        in_specs=[
            pl.BlockSpec((rows, wide), lambda i: (i, 0)),
            pl.BlockSpec((rows, wide), lambda i: (i, 0)),
            pl.BlockSpec((1, ROWS), lambda i: (0, 0)),
        ],
        out_specs=pl.BlockSpec((N_TGT, rows, 2 * LANES), lambda i: (0, i, 0)),
        scratch_shapes=[pltpu.VMEM((rows, wide), BF)],
        compiler_params=pltpu.CompilerParams(vmem_limit_bytes=60 * 2**20),
        cost_estimate=pl.CostEstimate(
            flops=2 * ROWS * wide, bytes_accessed=8 * ROWS * wide, transcendentals=0
        ),
    )(flux, ivar, target)


def template_pair(templ_bf):
    none = jnp.zeros_like(templ_bf)
    return jnp.concatenate(
        [
            jnp.concatenate([templ_bf, none], axis=1),
            jnp.concatenate([none, templ_bf], axis=1),
        ],
        axis=0,
    )


def coadd_rows(core, got_ref, low_ref, high_ref, spectra_ref):
    inside = lax.broadcasted_iota(jnp.int32, (512, LANES), 1) < PIX
    first = (core * 8).astype(F32)
    selector = jnp.concatenate(
        [
            low_ref[...]
            * jnp.where(high_ref[0:1, :] == first + float(half * 16 + i), 1.0, 0.0).astype(BF)
            for half in range(2)
            for i in range(8)
        ],
        axis=0,
    )
    sums = jnp.dot(selector, got_ref[...], preferred_element_type=F32)
    coadd = sums[:, 0:LANES] / (sums[:, LANES:] + PRIOR_IVAR)
    for half in range(2):
        spectra_ref[:, half * LANES:(half + 1) * LANES] = jnp.where(
            inside, coadd[half * 512:(half + 1) * 512, :], 0.0
        ).astype(BF)


def away_body(core_ref, got_ref, away_ref, low_ref, high_ref):
    lane = lax.broadcasted_iota(jnp.int32, (16, LANES), 1)
    row = lax.broadcasted_iota(jnp.int32, (16, LANES), 0)
    pick = jnp.where(lane == PIX + row, 1.0, 0.0)
    pick = jnp.where(row < 2, pick, 0.0).astype(BF)
    ids = lax.dot_general(pick, got_ref[:, 0:LANES], NT, preferred_element_type=F32)
    high_ref[...] = jnp.broadcast_to(ids[0:1, :], high_ref.shape)
    low = ids[1:2, :].astype(jnp.int32)
    low_ref[...] = jnp.where(
        low == lax.broadcasted_iota(jnp.int32, low_ref.shape, 0), 1.0, 0.0
    ).astype(BF)
    coadd_rows(1 - core_ref[0], got_ref, low_ref, high_ref, away_ref)


def keep_body(core_ref, got_ref, low_ref, high_ref, keep_ref):
    coadd_rows(core_ref[0], got_ref, low_ref, high_ref, keep_ref)


def cross_of(keep_ref, came_ref, own_bf, other_bf):
    return lax.dot_general(
        keep_ref[...], template_pair(own_bf), NT, preferred_element_type=F32
    ) + lax.dot_general(
        came_ref[...], template_pair(other_bf), NT, preferred_element_type=F32
    )


def spread(value, lane):
    width = value.shape[1]
    wide = jnp.concatenate(
        [value, jnp.zeros((value.shape[0], LANES - width), F32)], axis=1
    )
    return wide if lane == 0 else pltpu.roll(wide, lane, 1)


def pack_gram(gram):
    top = spread(gram[0:16, :], 0) + spread(gram[16:32, :], 64)
    corner = gram[32:64, 32:64]
    low = sum(spread(corner[8 * i:8 * i + 8, :], 32 * i) for i in range(4))
    return jnp.concatenate([top, low], axis=0)


def unpack_gram(packed):
    top = jnp.concatenate(
        [packed[0:16, :], pltpu.roll(packed[0:16, :], 64, 1)], axis=0
    )[:, 0:RANK]
    low = packed[16:24, :]
    corner = jnp.concatenate(
        [low] + [pltpu.roll(low, LANES - 32 * i, 1) for i in range(1, 4)], axis=0
    )
    side = pad_to(top, LANES, LANES).T[32:64, :]
    lane = lax.broadcasted_iota(jnp.int32, (32, LANES), 1)
    bottom = jnp.where(lane < 32, side, pltpu.roll(corner, 32, 1))
    return jnp.concatenate([top, bottom[:, 0:RANK]], axis=0)


def exact(left, right):
    return jnp.dot(left, right, precision=lax.Precision.HIGHEST, preferred_element_type=F32)


def descend(state, residual, gram):
    eye = lax.broadcasted_iota(jnp.int32, (RANK, RANK), 0) == lax.broadcasted_iota(
        jnp.int32, (RANK, RANK), 1
    )
    pivot = jnp.sum(jnp.where(eye, gram, 0.0), axis=1, keepdims=True) + EPSILON
    inverse = 1.0 / pivot
    goal = state + residual * inverse
    scaled = gram * inverse
    goals = [goal[8 * i:8 * i + 8, :] for i in range(8)]
    done = []
    for k in range(RANK):
        old = state[k:k + 1, :]
        new = jnp.maximum(goals[k // 8][k % 8:k % 8 + 1, :], 0.0)
        done.append(new)
        change = new - old
        for i in range(k // 8, 8):
            goals[i] = goals[i] - scaled[8 * i:8 * i + 8, k:k + 1] * change
    return jnp.concatenate(done, axis=0)


def pad_to(value, rows, lanes):
    if value.shape[1] < lanes:
        value = jnp.concatenate(
            [value, jnp.zeros((value.shape[0], lanes - value.shape[1]), F32)], axis=1
        )
    if value.shape[0] < rows:
        value = jnp.concatenate(
            [value, jnp.zeros((rows - value.shape[0], value.shape[1]), F32)], axis=0
        )
    return value


def activation_body(first, *refs):
    if first:
        cross_ref, gram_ref, state_ref, new_ref, out_ref = refs
    else:
        cross_ref, state_ref, new_ref, out_ref = refs
    total = jnp.sum(cross_ref[...].astype(F32), axis=0)
    cross = pad_to(total[0:16, :], LANES, LANES).T
    wanted = cross[0:64, :] + pltpu.roll(cross[64:128, :], 16, 1)
    gram = unpack_gram(gram_ref[...] if first else total[16:40, :])
    if first:
        state = pad_to(state_ref[...], LANES, LANES).T[0:RANK, :]
    else:
        state = state_ref[...]
    rest = state if first else state - state.astype(BF).astype(F32)
    updated = descend(state, wanted - exact(gram, rest), gram)
    new_ref[...] = updated
    both = jnp.concatenate([updated, pltpu.roll(updated, LANES - 16, 1)], axis=0).T
    out_ref[...] = jnp.broadcast_to(both[0:16, :].astype(BF)[None], out_ref.shape)


def project_body(activ_ref, keep_ref, came_ref, own_ref, send_ref):
    activ = activ_ref[...]
    gram = lax.dot_general(activ, activ, TN, preferred_element_type=F32)
    gram = pack_gram(gram[0:64, 0:64] + pltpu.roll(gram[64:128, :], 64, 1)[:, 0:64])
    blocks = []
    for ref in (keep_ref, came_ref):
        proj = lax.dot_general(activ, ref[...], TN, preferred_element_type=F32)
        blocks.append(proj[0:64, 0:LANES] + proj[64:128, LANES:])
    own_ref[0:24, :] = gram
    own_ref[24:88, :] = blocks[0]
    send_ref[0:24, :] = gram
    send_ref[24:88, :] = blocks[1]
    if own_ref.shape[0] > 88:
        own_ref[88:152, :] = blocks[1]
        send_ref[24:88, :] = blocks[1]
        send_ref[88:152, :] = blocks[0]


def new_templates(part_refs, templ):
    one, two, three, four = (ref[...] for ref in part_refs)
    total = (one + three) + (two + four)
    gram, proj = unpack_gram(total[0:24, :]), total[24:88, :]
    if total.shape[0] > 88:
        proj = jnp.concatenate([proj, total[88:152, :]], axis=1)
    return descend(templ, proj - exact(gram, templ), gram)


def template_body(a_ref, b_ref, c_ref, d_ref, own_ref, other_ref, activ_ref, keep_ref, came_ref, new_ref, out_ref):
    templ = jnp.concatenate([own_ref[...], other_ref[...]], axis=1)
    updated = new_templates((a_ref, b_ref, c_ref, d_ref), templ)
    new_ref[...] = updated[:, 0:LANES]
    templ_bf = updated.astype(BF)
    full = lax.dot_general(templ_bf, templ_bf, NT, preferred_element_type=F32)
    square = template_pair(full)
    high = square.astype(BF)
    low = (square - high.astype(F32)).astype(BF)
    rows = activ_ref[...]
    fitted = jnp.dot(rows, high, preferred_element_type=F32) + jnp.dot(
        rows, low, preferred_element_type=F32
    )
    cross = cross_of(keep_ref, came_ref, templ_bf[:, 0:LANES], templ_bf[:, LANES:]) - fitted
    gram = jnp.broadcast_to(pack_gram(full)[None], (32, 24, LANES))
    out_ref[...] = jnp.concatenate([cross.reshape(32, 16, LANES), gram], axis=1).astype(BF)


def last_template_body(a_ref, b_ref, c_ref, d_ref, templ_ref, state_ref, new_ref, activ_ref):
    activ_ref[...] = pad_to(state_ref[...], LANES, LANES).T[0:32, 0:RANK]
    updated = new_templates((a_ref, b_ref, c_ref, d_ref), templ_ref[...])
    new_ref[...] = updated[:, 0:PIX]


def first_gram_body(templ_ref, gram_ref):
    templ_bf = templ_ref[...].astype(BF)
    gram_ref[...] = pack_gram(
        lax.dot_general(templ_bf, templ_bf, NT, preferred_element_type=F32)
    )


def shift(value, axis, size, by):
    return lax.ppermute(value, axis, [(i, (i + by) % size) for i in range(size)])


def ring_sum(value, axis, size, step):
    return (value + shift(value, axis, size, 2 * step)) + (
        shift(value, axis, size, step) + shift(value, axis, size, 3 * step)
    )


def from_ahead(value, by):
    pairs = [
        ((z + 2 * y + by) % NZ * NY + y, z * NY + y) for z in range(NZ) for y in range(NY)
    ]
    return lax.ppermute(value, ("z", "y"), pairs)


def near(part):
    part = ring_sum(part + shift(part, "c", NC, 1), "x", NX, 1)
    return from_ahead(part, 0) + from_ahead(part, 1)


def first_message_body(own_ref, other_ref, keep_ref, came_ref, out_ref):
    cross = cross_of(keep_ref, came_ref, own_ref[...].astype(BF), other_ref[...].astype(BF))
    out_ref[...] = cross.reshape(32, 16, LANES)


def sds(*shape, dtype=F32):
    return jax.ShapeDtypeStruct(shape, dtype)


def shards(flux, ivar, row_target, start_w, start_h):
    core = lax.axis_index("c").astype(jnp.int32).reshape(1)
    send = pack(flux, ivar, row_target.reshape(1, ROWS))
    templates = jnp.pad(start_h, ((0, 0), (0, LANES - PIX)))
    got = lax.all_to_all(send, TGT, split_axis=0, concat_axis=0, tiled=True)
    gram = near(call(first_gram_body, sds(24, LANES), (templates,)))
    other = shift(templates, "c", NC, 1)
    got, gram, other = lax.optimization_barrier((got, gram, other))
    rows = got.reshape(N_TGT * ROWS, 2 * LANES)
    half = sds(512, 2 * LANES, dtype=BF)
    cost = 2 * 1024 * N_TGT * ROWS * 2 * LANES
    away, low, high = call(
        away_body,
        (half, sds(64, N_TGT * ROWS, dtype=BF), sds(8, N_TGT * ROWS)),
        (core, rows),
        scalars=1,
        flops=cost,
    )
    came = shift(away, "c", NC, 1)
    keep = call(keep_body, half, (core, rows, low, high), scalars=1, flops=cost)
    cross = call(
        first_message_body, sds(32, 16, LANES), (templates, other, keep, came)
    )
    cross, gram = lax.optimization_barrier((cross, gram))
    gram = ring_sum(gram, "y", NY, 1)
    state = start_w
    for sweep in range(SWEEPS):
        first = sweep == 0
        cross = lax.all_to_all(cross, ("x", "z"), split_axis=0, concat_axis=0, tiled=True)
        state, message = call(
            lambda *refs, first=first: activation_body(first, *refs),
            (sds(RANK, LANES), sds(32, 16, LANES, dtype=BF)),
            (cross, gram, state) if first else (cross, state),
        )
        activ = lax.all_to_all(message, ("x", "z"), split_axis=0, concat_axis=0, tiled=True)
        activ = activ.reshape(512, LANES)
        size = 152 if first else 88
        part, away = call(
            project_body, (sds(size, LANES), sds(size, LANES)), (activ, keep, came)
        )
        part = part + shift(away, "c", NC, 1)
        parts = (part, *(shift(part, "y", NY, by) for by in (1, 2, 3)))
        if first:
            templates, cross = call(
                template_body,
                (sds(RANK, LANES), sds(32, 40, LANES, dtype=BF)),
                (*parts, templates, other, activ, keep, came),
            )
        else:
            templates, state = call(
                last_template_body,
                (sds(RANK, PIX), sds(32, RANK)),
                (*parts, templates, state),
            )
    return state, templates


def solution(mesh):
    grid = Mesh(mesh.devices.reshape(NX, NZ, NC, NY), ("x", "z", "c", "y"))
    every = ("x", "z", "c", "y")
    return jax.shard_map(
        shards,
        mesh=grid,
        in_specs=(P(every, None), P(every, None), P(every), P(every, None), P(None, TGT)),
        out_specs=(P(every, None), P(None, TGT)),
        check_vma=False,
    )
```

```python
import jax
import jax.numpy as jnp
from jax import lax
from jax.experimental import pallas as pl
from jax.experimental.pallas import tpu as pltpu
from jax.sharding import Mesh, PartitionSpec as P

SWEEPS = 2
PRIOR_IVAR = 0.5
EPSILON = 1e-06

NX, NZ, NC, NY = 4, 8, 2, 4
N_TGT = NX * NZ * NC
ROWS = 64
RANK = 64
PIX = 122
LANES = 128
TGT = ("x", "z", "c")
BF = jnp.bfloat16
F32 = jnp.float32
VMEM = pl.BlockSpec(memory_space=pltpu.VMEM)
SMEM = pl.BlockSpec(memory_space=pltpu.SMEM)
NT = (((1,), (1,)), ((), ()))
TN = (((0,), (0,)), ((), ()))


def call(body, outs, args, scratch=(), scalars=0, flops=0):
    return pl.pallas_call(
        body,
        out_shape=outs,
        in_specs=[SMEM] * scalars + [VMEM] * (len(args) - scalars),
        out_specs=jax.tree.map(lambda _: VMEM, outs),
        scratch_shapes=list(scratch),
        compiler_params=pltpu.CompilerParams(vmem_limit_bytes=40 * 2**20),
        cost_estimate=pl.CostEstimate(flops=flops, bytes_accessed=0, transcendentals=0)
        if flops
        else None,
    )(*args)


def pack_body(flux_ref, ivar_ref, target_ref, send_ref, weighted_ref):
    weighted_ref[...] = (
        ivar_ref[...].astype(F32) * flux_ref[...].astype(F32)
    ).astype(BF)
    rows = flux_ref.shape[0]
    at = lax.broadcasted_iota(jnp.int32, (rows, ROWS), 0) + pl.program_id(0) * rows
    here = at == lax.broadcasted_iota(jnp.int32, (rows, ROWS), 1)
    target = jnp.where(here, jnp.broadcast_to(target_ref[...], (rows, ROWS)), 0)
    target = jnp.broadcast_to(jnp.sum(target, axis=1, keepdims=True), (rows, LANES))
    peer, local = target // 128, target % 32
    chip = peer // 2 % NZ * NX + peer // 16
    index = (local // 16) * 1024 + (peer % 2) * 512 + chip * 16 + local % 16
    lane = lax.broadcasted_iota(jnp.int32, (rows, LANES), 1)
    extra = jnp.where(lane == 0, index // 64, jnp.where(lane == 1, index % 64, 0))
    extra = extra.astype(F32).astype(BF)
    for dev in range(N_TGT):
        span = slice(dev * PIX, dev * PIX + PIX)
        send_ref[dev, :, 0:PIX] = weighted_ref[:, span]
        send_ref[dev, :, PIX:LANES] = extra[:, 0:LANES - PIX]
        send_ref[dev, :, LANES:LANES + PIX] = ivar_ref[:, span]
        send_ref[dev, :, LANES + PIX:2 * LANES] = jnp.zeros((rows, LANES - PIX), BF)


def pack(flux, ivar, target):
    rows, wide = 32, flux.shape[1]
    return pl.pallas_call(
        pack_body,
        grid=(ROWS // rows,),
        out_shape=sds(N_TGT, ROWS, 2 * LANES, dtype=BF),
        in_specs=[
            pl.BlockSpec((rows, wide), lambda i: (i, 0)),
            pl.BlockSpec((rows, wide), lambda i: (i, 0)),
            pl.BlockSpec((1, ROWS), lambda i: (0, 0)),
        ],
        out_specs=pl.BlockSpec((N_TGT, rows, 2 * LANES), lambda i: (0, i, 0)),
        scratch_shapes=[pltpu.VMEM((rows, wide), BF)],
        compiler_params=pltpu.CompilerParams(vmem_limit_bytes=60 * 2**20),
        cost_estimate=pl.CostEstimate(
            flops=2 * ROWS * wide, bytes_accessed=8 * ROWS * wide, transcendentals=0
        ),
    )(flux, ivar, target)


def template_pair(templ_bf):
    none = jnp.zeros_like(templ_bf)
    return jnp.concatenate(
        [
            jnp.concatenate([templ_bf, none], axis=1),
            jnp.concatenate([none, templ_bf], axis=1),
        ],
        axis=0,
    )


def coadd_rows(core, got_ref, low_ref, high_ref, spectra_ref):
    inside = lax.broadcasted_iota(jnp.int32, (512, LANES), 1) < PIX
    first = (core * 8).astype(F32)
    selector = jnp.concatenate(
        [
            low_ref[...]
            * jnp.where(high_ref[0:1, :] == first + float(half * 16 + i), 1.0, 0.0).astype(BF)
            for half in range(2)
            for i in range(8)
        ],
        axis=0,
    )
    sums = jnp.dot(selector, got_ref[...], preferred_element_type=F32)
    coadd = sums[:, 0:LANES] / (sums[:, LANES:] + PRIOR_IVAR)
    for half in range(2):
        spectra_ref[:, half * LANES:(half + 1) * LANES] = jnp.where(
            inside, coadd[half * 512:(half + 1) * 512, :], 0.0
        ).astype(BF)


def away_body(core_ref, got_ref, away_ref, low_ref, high_ref):
    lane = lax.broadcasted_iota(jnp.int32, (16, LANES), 1)
    row = lax.broadcasted_iota(jnp.int32, (16, LANES), 0)
    pick = jnp.where(lane == PIX + row, 1.0, 0.0)
    pick = jnp.where(row < 2, pick, 0.0).astype(BF)
    ids = lax.dot_general(pick, got_ref[:, 0:LANES], NT, preferred_element_type=F32)
    high_ref[...] = jnp.broadcast_to(ids[0:1, :], high_ref.shape)
    low = ids[1:2, :].astype(jnp.int32)
    low_ref[...] = jnp.where(
        low == lax.broadcasted_iota(jnp.int32, low_ref.shape, 0), 1.0, 0.0
    ).astype(BF)
    coadd_rows(1 - core_ref[0], got_ref, low_ref, high_ref, away_ref)


def keep_body(core_ref, got_ref, low_ref, high_ref, keep_ref):
    coadd_rows(core_ref[0], got_ref, low_ref, high_ref, keep_ref)


def cross_of(keep_ref, came_ref, own_bf, other_bf):
    return lax.dot_general(
        keep_ref[...], template_pair(own_bf), NT, preferred_element_type=F32
    ) + lax.dot_general(
        came_ref[...], template_pair(other_bf), NT, preferred_element_type=F32
    )


def spread(value, lane):
    width = value.shape[1]
    wide = jnp.concatenate(
        [value, jnp.zeros((value.shape[0], LANES - width), F32)], axis=1
    )
    return wide if lane == 0 else pltpu.roll(wide, lane, 1)


def pack_gram(gram):
    top = spread(gram[0:16, :], 0) + spread(gram[16:32, :], 64)
    corner = gram[32:64, 32:64]
    low = sum(spread(corner[8 * i:8 * i + 8, :], 32 * i) for i in range(4))
    return jnp.concatenate([top, low], axis=0)


def unpack_gram(packed):
    top = jnp.concatenate(
        [packed[0:16, :], pltpu.roll(packed[0:16, :], 64, 1)], axis=0
    )[:, 0:RANK]
    low = packed[16:24, :]
    corner = jnp.concatenate(
        [low] + [pltpu.roll(low, LANES - 32 * i, 1) for i in range(1, 4)], axis=0
    )
    side = pad_to(top, LANES, LANES).T[32:64, :]
    lane = lax.broadcasted_iota(jnp.int32, (32, LANES), 1)
    bottom = jnp.where(lane < 32, side, pltpu.roll(corner, 32, 1))
    return jnp.concatenate([top, bottom[:, 0:RANK]], axis=0)


def exact(left, right):
    return jnp.dot(left, right, precision=lax.Precision.HIGHEST, preferred_element_type=F32)


def descend(state, residual, gram):
    eye = lax.broadcasted_iota(jnp.int32, (RANK, RANK), 0) == lax.broadcasted_iota(
        jnp.int32, (RANK, RANK), 1
    )
    pivot = jnp.sum(jnp.where(eye, gram, 0.0), axis=1, keepdims=True) + EPSILON
    inverse = 1.0 / pivot
    goal = state + residual * inverse
    scaled = gram * inverse
    goals = [goal[8 * i:8 * i + 8, :] for i in range(8)]
    done = []
    for k in range(RANK):
        old = state[k:k + 1, :]
        new = jnp.maximum(goals[k // 8][k % 8:k % 8 + 1, :], 0.0)
        done.append(new)
        change = new - old
        for i in range(k // 8, 8):
            goals[i] = goals[i] - scaled[8 * i:8 * i + 8, k:k + 1] * change
    return jnp.concatenate(done, axis=0)


def pad_to(value, rows, lanes):
    if value.shape[1] < lanes:
        value = jnp.concatenate(
            [value, jnp.zeros((value.shape[0], lanes - value.shape[1]), F32)], axis=1
        )
    if value.shape[0] < rows:
        value = jnp.concatenate(
            [value, jnp.zeros((rows - value.shape[0], value.shape[1]), F32)], axis=0
        )
    return value


def activation_body(first, *refs):
    if first:
        cross_ref, gram_ref, state_ref, new_ref, out_ref = refs
    else:
        cross_ref, state_ref, new_ref, out_ref = refs
    total = jnp.sum(cross_ref[...].astype(F32), axis=0)
    cross = pad_to(total[0:16, :], LANES, LANES).T
    wanted = cross[0:64, :] + pltpu.roll(cross[64:128, :], 16, 1)
    gram = unpack_gram(gram_ref[...] if first else total[16:40, :])
    if first:
        state = pad_to(state_ref[...], LANES, LANES).T[0:RANK, :]
    else:
        state = state_ref[...]
    rest = state if first else state - state.astype(BF).astype(F32)
    updated = descend(state, wanted - exact(gram, rest), gram)
    new_ref[...] = updated
    both = jnp.concatenate([updated, pltpu.roll(updated, LANES - 16, 1)], axis=0).T
    out_ref[...] = jnp.broadcast_to(both[0:16, :].astype(BF)[None], out_ref.shape)


def project_body(activ_ref, keep_ref, came_ref, own_ref, send_ref):
    activ = activ_ref[...]
    gram = lax.dot_general(activ, activ, TN, preferred_element_type=F32)
    gram = pack_gram(gram[0:64, 0:64] + pltpu.roll(gram[64:128, :], 64, 1)[:, 0:64])
    blocks = []
    for ref in (keep_ref, came_ref):
        proj = lax.dot_general(activ, ref[...], TN, preferred_element_type=F32)
        blocks.append(proj[0:64, 0:LANES] + proj[64:128, LANES:])
    own_ref[0:24, :] = gram
    own_ref[24:88, :] = blocks[0]
    send_ref[0:24, :] = gram
    send_ref[24:88, :] = blocks[1]
    if own_ref.shape[0] > 88:
        own_ref[88:152, :] = blocks[1]
        send_ref[24:88, :] = blocks[1]
        send_ref[88:152, :] = blocks[0]


def new_templates(part_refs, templ):
    one, two, three, four = (ref[...] for ref in part_refs)
    total = (one + three) + (two + four)
    gram, proj = unpack_gram(total[0:24, :]), total[24:88, :]
    if total.shape[0] > 88:
        proj = jnp.concatenate([proj, total[88:152, :]], axis=1)
    return descend(templ, proj - exact(gram, templ), gram)


def template_body(a_ref, b_ref, c_ref, d_ref, own_ref, other_ref, activ_ref, keep_ref, came_ref, new_ref, out_ref):
    templ = jnp.concatenate([own_ref[...], other_ref[...]], axis=1)
    updated = new_templates((a_ref, b_ref, c_ref, d_ref), templ)
    new_ref[...] = updated[:, 0:LANES]
    templ_bf = updated.astype(BF)
    full = lax.dot_general(templ_bf, templ_bf, NT, preferred_element_type=F32)
    square = template_pair(full)
    high = square.astype(BF)
    low = (square - high.astype(F32)).astype(BF)
    rows = activ_ref[...]
    fitted = jnp.dot(rows, high, preferred_element_type=F32) + jnp.dot(
        rows, low, preferred_element_type=F32
    )
    cross = cross_of(keep_ref, came_ref, templ_bf[:, 0:LANES], templ_bf[:, LANES:]) - fitted
    gram = jnp.broadcast_to(pack_gram(full)[None], (32, 24, LANES))
    out_ref[...] = jnp.concatenate([cross.reshape(32, 16, LANES), gram], axis=1).astype(BF)


def last_template_body(a_ref, b_ref, c_ref, d_ref, templ_ref, state_ref, new_ref, activ_ref):
    activ_ref[...] = pad_to(state_ref[...], LANES, LANES).T[0:32, 0:RANK]
    updated = new_templates((a_ref, b_ref, c_ref, d_ref), templ_ref[...])
    new_ref[...] = updated[:, 0:PIX]


def first_gram_body(templ_ref, gram_ref):
    templ_bf = templ_ref[...].astype(BF)
    gram_ref[...] = pack_gram(
        lax.dot_general(templ_bf, templ_bf, NT, preferred_element_type=F32)
    )


def shift(value, axis, size, by):
    return lax.ppermute(value, axis, [(i, (i + by) % size) for i in range(size)])


def ring_sum(value, axis, size, step):
    return (value + shift(value, axis, size, 2 * step)) + (
        shift(value, axis, size, step) + shift(value, axis, size, 3 * step)
    )


def from_ahead(value, by):
    pairs = [
        ((z + 2 * y + by) % NZ * NY + y, z * NY + y) for z in range(NZ) for y in range(NY)
    ]
    return lax.ppermute(value, ("z", "y"), pairs)


def near(part):
    part = ring_sum(part + shift(part, "c", NC, 1), "x", NX, 1)
    return from_ahead(part, 0) + from_ahead(part, 1)


def first_message_body(own_ref, other_ref, keep_ref, came_ref, out_ref):
    cross = cross_of(keep_ref, came_ref, own_ref[...].astype(BF), other_ref[...].astype(BF))
    out_ref[...] = cross.reshape(32, 16, LANES)


def sds(*shape, dtype=F32):
    return jax.ShapeDtypeStruct(shape, dtype)


def shards(flux, ivar, row_target, start_w, start_h):
    core = lax.axis_index("c").astype(jnp.int32).reshape(1)
    send = pack(flux, ivar, row_target.reshape(1, ROWS))
    templates = jnp.pad(start_h, ((0, 0), (0, LANES - PIX)))
    got = lax.all_to_all(send, TGT, split_axis=0, concat_axis=0, tiled=True)
    gram = near(call(first_gram_body, sds(24, LANES), (templates,)))
    other = shift(templates, "c", NC, 1)
    got, gram, other = lax.optimization_barrier((got, gram, other))
    rows = got.reshape(N_TGT * ROWS, 2 * LANES)
    half = sds(512, 2 * LANES, dtype=BF)
    cost = 2 * 1024 * N_TGT * ROWS * 2 * LANES
    away, low, high = call(
        away_body,
        (half, sds(64, N_TGT * ROWS, dtype=BF), sds(8, N_TGT * ROWS)),
        (core, rows),
        scalars=1,
        flops=cost,
    )
    came = shift(away, "c", NC, 1)
    keep = call(keep_body, half, (core, rows, low, high), scalars=1, flops=cost)
    cross = call(
        first_message_body, sds(32, 16, LANES), (templates, other, keep, came)
    )
    cross, gram = lax.optimization_barrier((cross, gram))
    gram = ring_sum(gram, "y", NY, 1)
    state = start_w
    for sweep in range(SWEEPS):
        first = sweep == 0
        cross = lax.all_to_all(cross, ("z", "x"), split_axis=0, concat_axis=0, tiled=True)
        state, message = call(
            lambda *refs, first=first: activation_body(first, *refs),
            (sds(RANK, LANES), sds(32, 16, LANES, dtype=BF)),
            (cross, gram, state) if first else (cross, state),
        )
        activ = lax.all_to_all(message, ("z", "x"), split_axis=0, concat_axis=0, tiled=True)
        activ = activ.reshape(512, LANES)
        size = 152 if first else 88
        part, away = call(
            project_body, (sds(size, LANES), sds(size, LANES)), (activ, keep, came)
        )
        part = part + shift(away, "c", NC, 1)
        parts = (part, *(shift(part, "y", NY, by) for by in (1, 2, 3)))
        if first:
            templates, cross = call(
                template_body,
                (sds(RANK, LANES), sds(32, 40, LANES, dtype=BF)),
                (*parts, templates, other, activ, keep, came),
            )
        else:
            templates, state = call(
                last_template_body,
                (sds(RANK, PIX), sds(32, RANK)),
                (*parts, templates, state),
            )
    return state, templates


def solution(mesh):
    grid = Mesh(mesh.devices.reshape(NX, NZ, NC, NY), ("x", "z", "c", "y"))
    every = ("x", "z", "c", "y")
    return jax.shard_map(
        shards,
        mesh=grid,
        in_specs=(P(every, None), P(every, None), P(every), P(every, None), P(None, TGT)),
        out_specs=(P(every, None), P(None, TGT)),
        check_vma=False,
    )
```

```python
import jax
import jax.numpy as jnp
from jax import lax
from jax.experimental import pallas as pl
from jax.experimental.pallas import tpu as pltpu
from jax.sharding import Mesh, PartitionSpec as P

SWEEPS = 2
PRIOR_IVAR = 0.5
EPSILON = 1e-06

NX, NZ, NC, NY = 4, 8, 2, 4
N_TGT = NX * NZ * NC
ROWS = 64
RANK = 64
PIX = 122
LANES = 128
TGT = ("x", "z", "c")
BF = jnp.bfloat16
F32 = jnp.float32
VMEM = pl.BlockSpec(memory_space=pltpu.VMEM)
SMEM = pl.BlockSpec(memory_space=pltpu.SMEM)
NT = (((1,), (1,)), ((), ()))
TN = (((0,), (0,)), ((), ()))


def call(body, outs, args, scratch=(), scalars=0, flops=0):
    return pl.pallas_call(
        body,
        out_shape=outs,
        in_specs=[SMEM] * scalars + [VMEM] * (len(args) - scalars),
        out_specs=jax.tree.map(lambda _: VMEM, outs),
        scratch_shapes=list(scratch),
        compiler_params=pltpu.CompilerParams(vmem_limit_bytes=40 * 2**20),
        cost_estimate=pl.CostEstimate(flops=flops, bytes_accessed=0, transcendentals=0)
        if flops
        else None,
    )(*args)


def pack_body(flux_ref, ivar_ref, target_ref, send_ref, weighted_ref):
    weighted_ref[...] = (
        ivar_ref[...].astype(F32) * flux_ref[...].astype(F32)
    ).astype(BF)
    rows = flux_ref.shape[0]
    at = lax.broadcasted_iota(jnp.int32, (rows, ROWS), 0) + pl.program_id(0) * rows
    here = at == lax.broadcasted_iota(jnp.int32, (rows, ROWS), 1)
    target = jnp.where(here, jnp.broadcast_to(target_ref[...], (rows, ROWS)), 0)
    target = jnp.broadcast_to(jnp.sum(target, axis=1, keepdims=True), (rows, LANES))
    peer, local = target // 128, target % 32
    index = (local // 16) * 1024 + (peer % 2) * 512 + (peer // 2) * 16 + local % 16
    lane = lax.broadcasted_iota(jnp.int32, (rows, LANES), 1)
    extra = jnp.where(lane == 0, index // 64, jnp.where(lane == 1, index % 64, 0))
    extra = extra.astype(F32).astype(BF)
    for dev in range(N_TGT):
        span = slice(dev * PIX, dev * PIX + PIX)
        send_ref[dev, :, 0:PIX] = weighted_ref[:, span]
        send_ref[dev, :, PIX:LANES] = extra[:, 0:LANES - PIX]
        send_ref[dev, :, LANES:LANES + PIX] = ivar_ref[:, span]
        send_ref[dev, :, LANES + PIX:2 * LANES] = jnp.zeros((rows, LANES - PIX), BF)


def pack(flux, ivar, target):
    rows, wide = 32, flux.shape[1]
    return pl.pallas_call(
        pack_body,
        grid=(ROWS // rows,),
        out_shape=sds(N_TGT, ROWS, 2 * LANES, dtype=BF),
        in_specs=[
            pl.BlockSpec((rows, wide), lambda i: (i, 0)),
            pl.BlockSpec((rows, wide), lambda i: (i, 0)),
            pl.BlockSpec((1, ROWS), lambda i: (0, 0)),
        ],
        out_specs=pl.BlockSpec((N_TGT, rows, 2 * LANES), lambda i: (0, i, 0)),
        scratch_shapes=[pltpu.VMEM((rows, wide), BF)],
        compiler_params=pltpu.CompilerParams(vmem_limit_bytes=60 * 2**20),
        cost_estimate=pl.CostEstimate(
            flops=2 * ROWS * wide, bytes_accessed=8 * ROWS * wide, transcendentals=0
        ),
    )(flux, ivar, target)


def template_pair(templ_bf):
    none = jnp.zeros_like(templ_bf)
    return jnp.concatenate(
        [
            jnp.concatenate([templ_bf, none], axis=1),
            jnp.concatenate([none, templ_bf], axis=1),
        ],
        axis=0,
    )


def coadd_rows(core, got_ref, low_ref, high_ref, spectra_ref):
    inside = lax.broadcasted_iota(jnp.int32, (512, LANES), 1) < PIX
    first = (core * 8).astype(F32)
    selector = jnp.concatenate(
        [
            low_ref[...]
            * jnp.where(high_ref[0:1, :] == first + float(half * 16 + i), 1.0, 0.0).astype(BF)
            for half in range(2)
            for i in range(8)
        ],
        axis=0,
    )
    sums = jnp.dot(selector, got_ref[...], preferred_element_type=F32)
    coadd = sums[:, 0:LANES] / (sums[:, LANES:] + PRIOR_IVAR)
    for half in range(2):
        spectra_ref[:, half * LANES:(half + 1) * LANES] = jnp.where(
            inside, coadd[half * 512:(half + 1) * 512, :], 0.0
        ).astype(BF)


def away_body(core_ref, got_ref, away_ref, low_ref, high_ref):
    lane = lax.broadcasted_iota(jnp.int32, (16, LANES), 1)
    row = lax.broadcasted_iota(jnp.int32, (16, LANES), 0)
    pick = jnp.where(lane == PIX + row, 1.0, 0.0)
    pick = jnp.where(row < 2, pick, 0.0).astype(BF)
    ids = lax.dot_general(pick, got_ref[:, 0:LANES], NT, preferred_element_type=F32)
    high_ref[...] = jnp.broadcast_to(ids[0:1, :], high_ref.shape)
    low = ids[1:2, :].astype(jnp.int32)
    low_ref[...] = jnp.where(
        low == lax.broadcasted_iota(jnp.int32, low_ref.shape, 0), 1.0, 0.0
    ).astype(BF)
    coadd_rows(1 - core_ref[0], got_ref, low_ref, high_ref, away_ref)


def keep_body(core_ref, got_ref, low_ref, high_ref, keep_ref):
    coadd_rows(core_ref[0], got_ref, low_ref, high_ref, keep_ref)


def cross_of(keep_ref, came_ref, own_bf, other_bf):
    return lax.dot_general(
        keep_ref[...], template_pair(own_bf), NT, preferred_element_type=F32
    ) + lax.dot_general(
        came_ref[...], template_pair(other_bf), NT, preferred_element_type=F32
    )


def spread(value, lane):
    width = value.shape[1]
    wide = jnp.concatenate(
        [value, jnp.zeros((value.shape[0], LANES - width), F32)], axis=1
    )
    return wide if lane == 0 else pltpu.roll(wide, lane, 1)


def pack_gram(gram):
    top = spread(gram[0:16, :], 0) + spread(gram[16:32, :], 64)
    corner = gram[32:64, 32:64]
    low = sum(spread(corner[8 * i:8 * i + 8, :], 32 * i) for i in range(4))
    return jnp.concatenate([top, low], axis=0)


def unpack_gram(packed):
    top = jnp.concatenate(
        [packed[0:16, :], pltpu.roll(packed[0:16, :], 64, 1)], axis=0
    )[:, 0:RANK]
    low = packed[16:24, :]
    corner = jnp.concatenate(
        [low] + [pltpu.roll(low, LANES - 32 * i, 1) for i in range(1, 4)], axis=0
    )
    side = pad_to(top, LANES, LANES).T[32:64, :]
    lane = lax.broadcasted_iota(jnp.int32, (32, LANES), 1)
    bottom = jnp.where(lane < 32, side, pltpu.roll(corner, 32, 1))
    return jnp.concatenate([top, bottom[:, 0:RANK]], axis=0)


def exact(left, right):
    return jnp.dot(left, right, precision=lax.Precision.HIGHEST, preferred_element_type=F32)


def descend(state, residual, gram):
    eye = lax.broadcasted_iota(jnp.int32, (RANK, RANK), 0) == lax.broadcasted_iota(
        jnp.int32, (RANK, RANK), 1
    )
    pivot = jnp.sum(jnp.where(eye, gram, 0.0), axis=1, keepdims=True) + EPSILON
    inverse = 1.0 / pivot
    goal = state + residual * inverse
    scaled = gram * inverse
    goals = [goal[8 * i:8 * i + 8, :] for i in range(8)]
    done = []
    for k in range(RANK):
        old = state[k:k + 1, :]
        new = jnp.maximum(goals[k // 8][k % 8:k % 8 + 1, :], 0.0)
        done.append(new)
        change = new - old
        for i in range(k // 8, 8):
            goals[i] = goals[i] - scaled[8 * i:8 * i + 8, k:k + 1] * change
    return jnp.concatenate(done, axis=0)


def pad_to(value, rows, lanes):
    if value.shape[1] < lanes:
        value = jnp.concatenate(
            [value, jnp.zeros((value.shape[0], lanes - value.shape[1]), F32)], axis=1
        )
    if value.shape[0] < rows:
        value = jnp.concatenate(
            [value, jnp.zeros((rows - value.shape[0], value.shape[1]), F32)], axis=0
        )
    return value


def activation_body(first, *refs):
    if first:
        cross_ref, gram_ref, state_ref, new_ref, out_ref = refs
    else:
        cross_ref, state_ref, new_ref, out_ref = refs
    total = jnp.sum(cross_ref[...].astype(F32), axis=0)
    cross = pad_to(total[0:16, :], LANES, LANES).T
    wanted = cross[0:64, :] + pltpu.roll(cross[64:128, :], 16, 1)
    gram = unpack_gram(gram_ref[...] if first else total[16:40, :])
    if first:
        state = pad_to(state_ref[...], LANES, LANES).T[0:RANK, :]
    else:
        state = state_ref[...]
    rest = state if first else state - state.astype(BF).astype(F32)
    updated = descend(state, wanted - exact(gram, rest), gram)
    new_ref[...] = updated
    both = jnp.concatenate([updated, pltpu.roll(updated, LANES - 16, 1)], axis=0).T
    out_ref[...] = jnp.broadcast_to(both[0:16, :].astype(BF)[None], out_ref.shape)


def project_body(activ_ref, keep_ref, came_ref, own_ref, send_ref):
    activ = activ_ref[...]
    gram = lax.dot_general(activ, activ, TN, preferred_element_type=F32)
    gram = pack_gram(gram[0:64, 0:64] + pltpu.roll(gram[64:128, :], 64, 1)[:, 0:64])
    blocks = []
    for ref in (keep_ref, came_ref):
        proj = lax.dot_general(activ, ref[...], TN, preferred_element_type=F32)
        blocks.append(proj[0:64, 0:LANES] + proj[64:128, LANES:])
    own_ref[0:24, :] = gram
    own_ref[24:88, :] = blocks[0]
    send_ref[0:24, :] = gram
    send_ref[24:88, :] = blocks[1]
    if own_ref.shape[0] > 88:
        own_ref[88:152, :] = blocks[1]
        send_ref[24:88, :] = blocks[1]
        send_ref[88:152, :] = blocks[0]


def new_templates(part_refs, templ):
    one, two, three, four = (ref[...] for ref in part_refs)
    total = (one + three) + (two + four)
    gram, proj = unpack_gram(total[0:24, :]), total[24:88, :]
    if total.shape[0] > 88:
        proj = jnp.concatenate([proj, total[88:152, :]], axis=1)
    return descend(templ, proj - exact(gram, templ), gram)


def template_body(a_ref, b_ref, c_ref, d_ref, own_ref, other_ref, activ_ref, keep_ref, came_ref, new_ref, out_ref):
    templ = jnp.concatenate([own_ref[...], other_ref[...]], axis=1)
    updated = new_templates((a_ref, b_ref, c_ref, d_ref), templ)
    new_ref[...] = updated[:, 0:LANES]
    templ_bf = updated.astype(BF)
    full = lax.dot_general(templ_bf, templ_bf, NT, preferred_element_type=F32)
    square = template_pair(full)
    high = square.astype(BF)
    low = (square - high.astype(F32)).astype(BF)
    rows = activ_ref[...]
    fitted = jnp.dot(rows, high, preferred_element_type=F32) + jnp.dot(
        rows, low, preferred_element_type=F32
    )
    cross = cross_of(keep_ref, came_ref, templ_bf[:, 0:LANES], templ_bf[:, LANES:]) - fitted
    gram = jnp.broadcast_to(pack_gram(full)[None], (32, 24, LANES))
    out_ref[...] = jnp.concatenate([cross.reshape(32, 16, LANES), gram], axis=1).astype(BF)


def last_template_body(a_ref, b_ref, c_ref, d_ref, templ_ref, state_ref, new_ref, activ_ref):
    activ_ref[...] = pad_to(state_ref[...], LANES, LANES).T[0:32, 0:RANK]
    updated = new_templates((a_ref, b_ref, c_ref, d_ref), templ_ref[...])
    new_ref[...] = updated[:, 0:PIX]


def first_gram_body(templ_ref, gram_ref):
    templ_bf = templ_ref[...].astype(BF)
    gram_ref[...] = pack_gram(
        lax.dot_general(templ_bf, templ_bf, NT, preferred_element_type=F32)
    )


def shift(value, axis, size, by):
    return lax.ppermute(value, axis, [(i, (i + by) % size) for i in range(size)])


def ring_sum(value, axis, size, step):
    return (value + shift(value, axis, size, 2 * step)) + (
        shift(value, axis, size, step) + shift(value, axis, size, 3 * step)
    )


def from_ahead(value, by):
    pairs = [
        ((z + 4 * c + by) % NZ * NC + c, z * NC + c) for z in range(NZ) for c in range(NC)
    ]
    return lax.ppermute(value, ("z", "c"), pairs)


def near(part):
    part = ring_sum(part + shift(part, "c", NC, 1), "x", NX, 1)
    return sum(from_ahead(part, by) for by in range(4))


def first_message_body(own_ref, other_ref, keep_ref, came_ref, out_ref):
    cross = cross_of(keep_ref, came_ref, own_ref[...].astype(BF), other_ref[...].astype(BF))
    out_ref[...] = cross.reshape(32, 16, LANES)


def sds(*shape, dtype=F32):
    return jax.ShapeDtypeStruct(shape, dtype)


def shards(flux, ivar, row_target, start_w, start_h):
    core = lax.axis_index("c").astype(jnp.int32).reshape(1)
    send = pack(flux, ivar, row_target.reshape(1, ROWS))
    templates = jnp.pad(start_h, ((0, 0), (0, LANES - PIX)))
    got = lax.all_to_all(send, TGT, split_axis=0, concat_axis=0, tiled=True)
    gram = near(call(first_gram_body, sds(24, LANES), (templates,)))
    other = shift(templates, "c", NC, 1)
    got, gram, other = lax.optimization_barrier((got, gram, other))
    gram = gram + shift(gram, "c", NC, 1)
    rows = got.reshape(N_TGT * ROWS, 2 * LANES)
    half = sds(512, 2 * LANES, dtype=BF)
    cost = 2 * 1024 * N_TGT * ROWS * 2 * LANES
    away, low, high = call(
        away_body,
        (half, sds(64, N_TGT * ROWS, dtype=BF), sds(8, N_TGT * ROWS)),
        (core, rows),
        scalars=1,
        flops=cost,
    )
    came = shift(away, "c", NC, 1)
    keep = call(keep_body, half, (core, rows, low, high), scalars=1, flops=cost)
    cross = call(
        first_message_body, sds(32, 16, LANES), (templates, other, keep, came)
    )
    cross, gram = lax.optimization_barrier((cross, gram))
    state = start_w
    for sweep in range(SWEEPS):
        first = sweep == 0
        cross = lax.all_to_all(cross, ("x", "z"), split_axis=0, concat_axis=0, tiled=True)
        state, message = call(
            lambda *refs, first=first: activation_body(first, *refs),
            (sds(RANK, LANES), sds(32, 16, LANES, dtype=BF)),
            (cross, gram, state) if first else (cross, state),
        )
        activ = lax.all_to_all(message, ("x", "z"), split_axis=0, concat_axis=0, tiled=True)
        activ = activ.reshape(512, LANES)
        size = 152 if first else 88
        part, away = call(
            project_body, (sds(size, LANES), sds(size, LANES)), (activ, keep, came)
        )
        part = part + shift(away, "c", NC, 1)
        parts = (part, *(shift(part, "y", NY, by) for by in (1, 2, 3)))
        if first:
            templates, cross = call(
                template_body,
                (sds(RANK, LANES), sds(32, 40, LANES, dtype=BF)),
                (*parts, templates, other, activ, keep, came),
            )
        else:
            templates, state = call(
                last_template_body,
                (sds(RANK, PIX), sds(32, RANK)),
                (*parts, templates, state),
            )
    return state, templates


def solution(mesh):
    grid = Mesh(mesh.devices.reshape(NX, NZ, NC, NY), ("x", "z", "c", "y"))
    every = ("x", "z", "c", "y")
    return jax.shard_map(
        shards,
        mesh=grid,
        in_specs=(P(every, None), P(every, None), P(every), P(every, None), P(None, TGT)),
        out_specs=(P(every, None), P(None, TGT)),
        check_vma=False,
    )
```

```python
import jax
import jax.numpy as jnp
from jax import lax
from jax.experimental import pallas as pl
from jax.experimental.pallas import tpu as pltpu
from jax.sharding import Mesh, PartitionSpec as P

SWEEPS = 2
PRIOR_IVAR = 0.5
EPSILON = 1e-06

NX, NZ, NC, NY = 4, 8, 2, 4
N_TGT = NX * NZ * NC
ROWS = 64
RANK = 64
PIX = 122
LANES = 128
TGT = ("x", "z", "c")
BF = jnp.bfloat16
F32 = jnp.float32
VMEM = pl.BlockSpec(memory_space=pltpu.VMEM)
SMEM = pl.BlockSpec(memory_space=pltpu.SMEM)
NT = (((1,), (1,)), ((), ()))
TN = (((0,), (0,)), ((), ()))


def call(body, outs, args, scratch=(), scalars=0, flops=0):
    return pl.pallas_call(
        body,
        out_shape=outs,
        in_specs=[SMEM] * scalars + [VMEM] * (len(args) - scalars),
        out_specs=jax.tree.map(lambda _: VMEM, outs),
        scratch_shapes=list(scratch),
        compiler_params=pltpu.CompilerParams(vmem_limit_bytes=40 * 2**20),
        cost_estimate=pl.CostEstimate(flops=flops, bytes_accessed=0, transcendentals=0)
        if flops
        else None,
    )(*args)


def pack_body(flux_ref, ivar_ref, target_ref, send_ref, weighted_ref):
    weighted_ref[...] = (
        ivar_ref[...].astype(F32) * flux_ref[...].astype(F32)
    ).astype(BF)
    rows = flux_ref.shape[0]
    at = lax.broadcasted_iota(jnp.int32, (rows, ROWS), 0) + pl.program_id(0) * rows
    here = at == lax.broadcasted_iota(jnp.int32, (rows, ROWS), 1)
    target = jnp.where(here, jnp.broadcast_to(target_ref[...], (rows, ROWS)), 0)
    target = jnp.broadcast_to(jnp.sum(target, axis=1, keepdims=True), (rows, LANES))
    peer, local = target // 128, target % 32
    index = (local // 16) * 1024 + (peer % 2) * 512 + (peer // 2) * 16 + local % 16
    lane = lax.broadcasted_iota(jnp.int32, (rows, LANES), 1)
    extra = jnp.where(lane == 0, index // 64, jnp.where(lane == 1, index % 64, 0))
    extra = extra.astype(F32).astype(BF)
    for dev in range(N_TGT):
        span = slice(dev * PIX, dev * PIX + PIX)
        send_ref[dev, :, 0:PIX] = weighted_ref[:, span]
        send_ref[dev, :, PIX:LANES] = extra[:, 0:LANES - PIX]
        send_ref[dev, :, LANES:LANES + PIX] = ivar_ref[:, span]
        send_ref[dev, :, LANES + PIX:2 * LANES] = jnp.zeros((rows, LANES - PIX), BF)


def pack(flux, ivar, target):
    rows, wide = 32, flux.shape[1]
    return pl.pallas_call(
        pack_body,
        grid=(ROWS // rows,),
        out_shape=sds(N_TGT, ROWS, 2 * LANES, dtype=BF),
        in_specs=[
            pl.BlockSpec((rows, wide), lambda i: (i, 0)),
            pl.BlockSpec((rows, wide), lambda i: (i, 0)),
            pl.BlockSpec((1, ROWS), lambda i: (0, 0)),
        ],
        out_specs=pl.BlockSpec((N_TGT, rows, 2 * LANES), lambda i: (0, i, 0)),
        scratch_shapes=[pltpu.VMEM((rows, wide), BF)],
        compiler_params=pltpu.CompilerParams(vmem_limit_bytes=60 * 2**20),
        cost_estimate=pl.CostEstimate(
            flops=2 * ROWS * wide, bytes_accessed=8 * ROWS * wide, transcendentals=0
        ),
    )(flux, ivar, target)


def template_pair(templ_bf):
    none = jnp.zeros_like(templ_bf)
    return jnp.concatenate(
        [
            jnp.concatenate([templ_bf, none], axis=1),
            jnp.concatenate([none, templ_bf], axis=1),
        ],
        axis=0,
    )


def coadd_rows(core, got_ref, low_ref, high_ref, spectra_ref):
    inside = lax.broadcasted_iota(jnp.int32, (512, LANES), 1) < PIX
    first = (core * 8).astype(F32)
    selector = jnp.concatenate(
        [
            low_ref[...]
            * jnp.where(high_ref[0:1, :] == first + float(half * 16 + i), 1.0, 0.0).astype(BF)
            for half in range(2)
            for i in range(8)
        ],
        axis=0,
    )
    sums = jnp.dot(selector, got_ref[...], preferred_element_type=F32)
    coadd = sums[:, 0:LANES] / (sums[:, LANES:] + PRIOR_IVAR)
    for half in range(2):
        spectra_ref[:, half * LANES:(half + 1) * LANES] = jnp.where(
            inside, coadd[half * 512:(half + 1) * 512, :], 0.0
        ).astype(BF)


def away_body(core_ref, got_ref, away_ref, low_ref, high_ref):
    lane = lax.broadcasted_iota(jnp.int32, (16, LANES), 1)
    row = lax.broadcasted_iota(jnp.int32, (16, LANES), 0)
    pick = jnp.where(lane == PIX + row, 1.0, 0.0)
    pick = jnp.where(row < 2, pick, 0.0).astype(BF)
    ids = lax.dot_general(pick, got_ref[:, 0:LANES], NT, preferred_element_type=F32)
    high_ref[...] = jnp.broadcast_to(ids[0:1, :], high_ref.shape)
    low = ids[1:2, :].astype(jnp.int32)
    low_ref[...] = jnp.where(
        low == lax.broadcasted_iota(jnp.int32, low_ref.shape, 0), 1.0, 0.0
    ).astype(BF)
    coadd_rows(1 - core_ref[0], got_ref, low_ref, high_ref, away_ref)


def keep_body(core_ref, got_ref, low_ref, high_ref, keep_ref):
    coadd_rows(core_ref[0], got_ref, low_ref, high_ref, keep_ref)


def cross_of(keep_ref, came_ref, own_bf, other_bf):
    return lax.dot_general(
        keep_ref[...], template_pair(own_bf), NT, preferred_element_type=F32
    ) + lax.dot_general(
        came_ref[...], template_pair(other_bf), NT, preferred_element_type=F32
    )


def spread(value, lane):
    width = value.shape[1]
    wide = jnp.concatenate(
        [value, jnp.zeros((value.shape[0], LANES - width), F32)], axis=1
    )
    return wide if lane == 0 else pltpu.roll(wide, lane, 1)


def pack_gram(gram):
    top = spread(gram[0:16, :], 0) + spread(gram[16:32, :], 64)
    corner = gram[32:64, 32:64]
    low = sum(spread(corner[8 * i:8 * i + 8, :], 32 * i) for i in range(4))
    return jnp.concatenate([top, low], axis=0)


def unpack_gram(packed):
    top = jnp.concatenate(
        [packed[0:16, :], pltpu.roll(packed[0:16, :], 64, 1)], axis=0
    )[:, 0:RANK]
    low = packed[16:24, :]
    corner = jnp.concatenate(
        [low] + [pltpu.roll(low, LANES - 32 * i, 1) for i in range(1, 4)], axis=0
    )
    side = pad_to(top, LANES, LANES).T[32:64, :]
    lane = lax.broadcasted_iota(jnp.int32, (32, LANES), 1)
    bottom = jnp.where(lane < 32, side, pltpu.roll(corner, 32, 1))
    return jnp.concatenate([top, bottom[:, 0:RANK]], axis=0)


def exact(left, right):
    return jnp.dot(left, right, precision=lax.Precision.HIGHEST, preferred_element_type=F32)


def descend(state, residual, gram):
    eye = lax.broadcasted_iota(jnp.int32, (RANK, RANK), 0) == lax.broadcasted_iota(
        jnp.int32, (RANK, RANK), 1
    )
    pivot = jnp.sum(jnp.where(eye, gram, 0.0), axis=1, keepdims=True) + EPSILON
    inverse = 1.0 / pivot
    goal = state + residual * inverse
    scaled = gram * inverse
    goals = [goal[8 * i:8 * i + 8, :] for i in range(8)]
    done = []
    for k in range(RANK):
        old = state[k:k + 1, :]
        new = jnp.maximum(goals[k // 8][k % 8:k % 8 + 1, :], 0.0)
        done.append(new)
        change = new - old
        for i in range(k // 8, 8):
            goals[i] = goals[i] - scaled[8 * i:8 * i + 8, k:k + 1] * change
    return jnp.concatenate(done, axis=0)


def pad_to(value, rows, lanes):
    if value.shape[1] < lanes:
        value = jnp.concatenate(
            [value, jnp.zeros((value.shape[0], lanes - value.shape[1]), F32)], axis=1
        )
    if value.shape[0] < rows:
        value = jnp.concatenate(
            [value, jnp.zeros((rows - value.shape[0], value.shape[1]), F32)], axis=0
        )
    return value


def activation_body(first, *refs):
    if first:
        cross_ref, gram_ref, state_ref, new_ref, out_ref = refs
    else:
        cross_ref, state_ref, new_ref, out_ref = refs
    total = jnp.sum(cross_ref[...].astype(F32), axis=0)
    cross = pad_to(total[0:16, :], LANES, LANES).T
    wanted = cross[0:64, :] + pltpu.roll(cross[64:128, :], 16, 1)
    gram = unpack_gram(gram_ref[...] if first else total[16:40, :])
    if first:
        state = pad_to(state_ref[...], LANES, LANES).T[0:RANK, :]
    else:
        state = state_ref[...]
    rest = state if first else state - state.astype(BF).astype(F32)
    updated = descend(state, wanted - exact(gram, rest), gram)
    new_ref[...] = updated
    both = jnp.concatenate([updated, pltpu.roll(updated, LANES - 16, 1)], axis=0).T
    out_ref[...] = jnp.broadcast_to(both[0:16, :].astype(BF)[None], out_ref.shape)


def plain_gram(packed):
    return jnp.concatenate(
        [packed[:, 0:RANK], pltpu.roll(packed, RANK, 1)[:, 0:RANK]], axis=0
    )


def project(activ, spectra):
    proj = lax.dot_general(activ, spectra, TN, preferred_element_type=F32)
    return proj[0:64, 0:LANES] + proj[64:128, LANES:]


def activ_gram(activ):
    gram = lax.dot_general(activ, activ, TN, preferred_element_type=F32)
    gram = gram[0:64, 0:64] + pltpu.roll(gram[64:128, :], 64, 1)[:, 0:64]
    return spread(gram[0:32, :], 0) + spread(gram[32:64, :], 64)


def project_body(activ_ref, keep_ref, came_ref, own_ref, send_ref):
    activ = activ_ref[...]
    gram = activ_gram(activ)
    own, other = project(activ, keep_ref[...]), project(activ, came_ref[...])
    own_ref[0:32, :] = gram
    own_ref[32:96, :] = own
    own_ref[96:160, :] = other
    send_ref[0:32, :] = gram
    send_ref[32:96, :] = other
    send_ref[96:160, :] = own


def last_project_body(activ_ref, other_ref, keep_ref, away_ref, out_ref):
    activ, other = activ_ref[...], other_ref[...]
    out_ref[0:32, :] = activ_gram(activ) + activ_gram(other)
    out_ref[32:96, :] = project(activ, keep_ref[...]) + project(other, away_ref[...])


def new_templates(part_refs, templ):
    one, two, three, four = (ref[...] for ref in part_refs)
    total = (one + three) + (two + four)
    gram, proj = plain_gram(total[0:32, :]), total[32:96, :]
    if total.shape[0] > 96:
        proj = jnp.concatenate([proj, total[96:160, :]], axis=1)
    return descend(templ, proj - exact(gram, templ), gram)


def template_body(a_ref, b_ref, c_ref, d_ref, own_ref, other_ref, activ_ref, keep_ref, came_ref, new_ref, out_ref):
    templ = jnp.concatenate([own_ref[...], other_ref[...]], axis=1)
    updated = new_templates((a_ref, b_ref, c_ref, d_ref), templ)
    new_ref[...] = updated[:, 0:LANES]
    templ_bf = updated.astype(BF)
    full = lax.dot_general(templ_bf, templ_bf, NT, preferred_element_type=F32)
    square = template_pair(full)
    high = square.astype(BF)
    low = (square - high.astype(F32)).astype(BF)
    rows = activ_ref[...]
    fitted = jnp.dot(rows, high, preferred_element_type=F32) + jnp.dot(
        rows, low, preferred_element_type=F32
    )
    cross = cross_of(keep_ref, came_ref, templ_bf[:, 0:LANES], templ_bf[:, LANES:]) - fitted
    gram = jnp.broadcast_to(pack_gram(full)[None], (32, 24, LANES))
    out_ref[...] = jnp.concatenate([cross.reshape(32, 16, LANES), gram], axis=1).astype(BF)


def last_template_body(a_ref, b_ref, c_ref, d_ref, templ_ref, state_ref, new_ref, activ_ref):
    activ_ref[...] = pad_to(state_ref[...], LANES, LANES).T[0:32, 0:RANK]
    updated = new_templates((a_ref, b_ref, c_ref, d_ref), templ_ref[...])
    new_ref[...] = updated[:, 0:PIX]


def first_gram_body(templ_ref, gram_ref):
    templ_bf = templ_ref[...].astype(BF)
    gram_ref[...] = pack_gram(
        lax.dot_general(templ_bf, templ_bf, NT, preferred_element_type=F32)
    )


def shift(value, axis, size, by):
    return lax.ppermute(value, axis, [(i, (i + by) % size) for i in range(size)])


def ring_sum(value, axis, size, step):
    return (value + shift(value, axis, size, 2 * step)) + (
        shift(value, axis, size, step) + shift(value, axis, size, 3 * step)
    )


def from_ahead(value, by):
    pairs = [
        ((z + 4 * c + by) % NZ * NC + c, z * NC + c) for z in range(NZ) for c in range(NC)
    ]
    return lax.ppermute(value, ("z", "c"), pairs)


def near(part):
    part = ring_sum(part + shift(part, "c", NC, 1), "x", NX, 1)
    return sum(from_ahead(part, by) for by in range(4))


def first_message_body(own_ref, other_ref, keep_ref, came_ref, out_ref):
    cross = cross_of(keep_ref, came_ref, own_ref[...].astype(BF), other_ref[...].astype(BF))
    out_ref[...] = cross.reshape(32, 16, LANES)


def sds(*shape, dtype=F32):
    return jax.ShapeDtypeStruct(shape, dtype)


def shards(flux, ivar, row_target, start_w, start_h):
    core = lax.axis_index("c").astype(jnp.int32).reshape(1)
    send = pack(flux, ivar, row_target.reshape(1, ROWS))
    templates = jnp.pad(start_h, ((0, 0), (0, LANES - PIX)))
    got = lax.all_to_all(send, TGT, split_axis=0, concat_axis=0, tiled=True)
    gram = near(call(first_gram_body, sds(24, LANES), (templates,)))
    other = shift(templates, "c", NC, 1)
    got, gram, other = lax.optimization_barrier((got, gram, other))
    gram = gram + shift(gram, "c", NC, 1)
    rows = got.reshape(N_TGT * ROWS, 2 * LANES)
    half = sds(512, 2 * LANES, dtype=BF)
    cost = 2 * 1024 * N_TGT * ROWS * 2 * LANES
    away, low, high = call(
        away_body,
        (half, sds(64, N_TGT * ROWS, dtype=BF), sds(8, N_TGT * ROWS)),
        (core, rows),
        scalars=1,
        flops=cost,
    )
    came = shift(away, "c", NC, 1)
    keep = call(keep_body, half, (core, rows, low, high), scalars=1, flops=cost)
    cross = call(
        first_message_body, sds(32, 16, LANES), (templates, other, keep, came)
    )
    cross, gram = lax.optimization_barrier((cross, gram))
    state = start_w
    for sweep in range(SWEEPS):
        first = sweep == 0
        cross = lax.all_to_all(cross, ("x", "z"), split_axis=0, concat_axis=0, tiled=True)
        state, message = call(
            lambda *refs, first=first: activation_body(first, *refs),
            (sds(RANK, LANES), sds(32, 16, LANES, dtype=BF)),
            (cross, gram, state) if first else (cross, state),
        )
        activ = lax.all_to_all(message, ("x", "z"), split_axis=0, concat_axis=0, tiled=True)
        activ = activ.reshape(512, LANES)
        if first:
            both = (sds(160, LANES), sds(160, LANES))
            part, sent = call(project_body, both, (activ, keep, came))
            part = part + shift(sent, "c", NC, 1)
        else:
            part = call(
                last_project_body,
                sds(96, LANES),
                (activ, shift(activ, "c", NC, 1), keep, away),
            )
        parts = (part, *(shift(part, "y", NY, by) for by in (1, 2, 3)))
        if first:
            templates, cross = call(
                template_body,
                (sds(RANK, LANES), sds(32, 40, LANES, dtype=BF)),
                (*parts, templates, other, activ, keep, came),
            )
        else:
            templates, state = call(
                last_template_body,
                (sds(RANK, PIX), sds(32, RANK)),
                (*parts, templates, state),
            )
    return state, templates


def solution(mesh):
    grid = Mesh(mesh.devices.reshape(NX, NZ, NC, NY), ("x", "z", "c", "y"))
    every = ("x", "z", "c", "y")
    return jax.shard_map(
        shards,
        mesh=grid,
        in_specs=(P(every, None), P(every, None), P(every), P(every, None), P(None, TGT)),
        out_specs=(P(every, None), P(None, TGT)),
        check_vma=False,
    )
```

```python
import jax
import jax.numpy as jnp
from jax import lax
from jax.experimental import pallas as pl
from jax.experimental.pallas import tpu as pltpu
from jax.sharding import Mesh, PartitionSpec as P

SWEEPS = 2
PRIOR_IVAR = 0.5
EPSILON = 1e-06

NX, NZ, NC, NY = 4, 8, 2, 4
N_TGT = NX * NZ * NC
ROWS = 64
RANK = 64
PIX = 122
LANES = 128
TGT = ("x", "z", "c")
BF = jnp.bfloat16
F32 = jnp.float32
VMEM = pl.BlockSpec(memory_space=pltpu.VMEM)
SMEM = pl.BlockSpec(memory_space=pltpu.SMEM)
NT = (((1,), (1,)), ((), ()))
TN = (((0,), (0,)), ((), ()))


def call(body, outs, args, scratch=(), scalars=0, flops=0):
    return pl.pallas_call(
        body,
        out_shape=outs,
        in_specs=[SMEM] * scalars + [VMEM] * (len(args) - scalars),
        out_specs=jax.tree.map(lambda _: VMEM, outs),
        scratch_shapes=list(scratch),
        compiler_params=pltpu.CompilerParams(vmem_limit_bytes=40 * 2**20),
        cost_estimate=pl.CostEstimate(flops=flops, bytes_accessed=0, transcendentals=0)
        if flops
        else None,
    )(*args)


def pack_body(flux_ref, ivar_ref, target_ref, send_ref, weighted_ref):
    weighted_ref[...] = (
        ivar_ref[...].astype(F32) * flux_ref[...].astype(F32)
    ).astype(BF)
    rows = flux_ref.shape[0]
    at = lax.broadcasted_iota(jnp.int32, (rows, ROWS), 0) + pl.program_id(0) * rows
    here = at == lax.broadcasted_iota(jnp.int32, (rows, ROWS), 1)
    target = jnp.where(here, jnp.broadcast_to(target_ref[...], (rows, ROWS)), 0)
    target = jnp.broadcast_to(jnp.sum(target, axis=1, keepdims=True), (rows, LANES))
    peer, local = target // 128, target % 32
    index = (local // 16) * 1024 + (peer % 2) * 512 + (peer // 2) * 16 + local % 16
    lane = lax.broadcasted_iota(jnp.int32, (rows, LANES), 1)
    extra = jnp.where(lane == 0, index // 64, jnp.where(lane == 1, index % 64, 0))
    extra = extra.astype(F32).astype(BF)
    for dev in range(N_TGT):
        span = slice(dev * PIX, dev * PIX + PIX)
        send_ref[dev, :, 0:PIX] = weighted_ref[:, span]
        send_ref[dev, :, PIX:LANES] = extra[:, 0:LANES - PIX]
        send_ref[dev, :, LANES:LANES + PIX] = ivar_ref[:, span]
        send_ref[dev, :, LANES + PIX:2 * LANES] = jnp.zeros((rows, LANES - PIX), BF)


def pack(flux, ivar, target):
    rows, wide = 32, flux.shape[1]
    return pl.pallas_call(
        pack_body,
        grid=(ROWS // rows,),
        out_shape=sds(N_TGT, ROWS, 2 * LANES, dtype=BF),
        in_specs=[
            pl.BlockSpec((rows, wide), lambda i: (i, 0)),
            pl.BlockSpec((rows, wide), lambda i: (i, 0)),
            pl.BlockSpec((1, ROWS), lambda i: (0, 0)),
        ],
        out_specs=pl.BlockSpec((N_TGT, rows, 2 * LANES), lambda i: (0, i, 0)),
        scratch_shapes=[pltpu.VMEM((rows, wide), BF)],
        compiler_params=pltpu.CompilerParams(vmem_limit_bytes=60 * 2**20),
        cost_estimate=pl.CostEstimate(
            flops=2 * ROWS * wide, bytes_accessed=8 * ROWS * wide, transcendentals=0
        ),
    )(flux, ivar, target)


def template_pair(templ_bf):
    none = jnp.zeros_like(templ_bf)
    return jnp.concatenate(
        [
            jnp.concatenate([templ_bf, none], axis=1),
            jnp.concatenate([none, templ_bf], axis=1),
        ],
        axis=0,
    )


def coadd_rows(core, got_ref, low_ref, high_ref, spectra_ref):
    inside = lax.broadcasted_iota(jnp.int32, (512, LANES), 1) < PIX
    first = (core * 8).astype(F32)
    selector = jnp.concatenate(
        [
            low_ref[...]
            * jnp.where(high_ref[0:1, :] == first + float(half * 16 + i), 1.0, 0.0).astype(BF)
            for half in range(2)
            for i in range(8)
        ],
        axis=0,
    )
    sums = jnp.dot(selector, got_ref[...], preferred_element_type=F32)
    coadd = sums[:, 0:LANES] / (sums[:, LANES:] + PRIOR_IVAR)
    for half in range(2):
        spectra_ref[:, half * LANES:(half + 1) * LANES] = jnp.where(
            inside, coadd[half * 512:(half + 1) * 512, :], 0.0
        ).astype(BF)


def away_body(core_ref, got_ref, away_ref, low_ref, high_ref):
    lane = lax.broadcasted_iota(jnp.int32, (16, LANES), 1)
    row = lax.broadcasted_iota(jnp.int32, (16, LANES), 0)
    pick = jnp.where(lane == PIX + row, 1.0, 0.0)
    pick = jnp.where(row < 2, pick, 0.0).astype(BF)
    ids = lax.dot_general(pick, got_ref[:, 0:LANES], NT, preferred_element_type=F32)
    high_ref[...] = jnp.broadcast_to(ids[0:1, :], high_ref.shape)
    low = ids[1:2, :].astype(jnp.int32)
    low_ref[...] = jnp.where(
        low == lax.broadcasted_iota(jnp.int32, low_ref.shape, 0), 1.0, 0.0
    ).astype(BF)
    coadd_rows(1 - core_ref[0], got_ref, low_ref, high_ref, away_ref)


def keep_body(core_ref, got_ref, low_ref, high_ref, keep_ref):
    coadd_rows(core_ref[0], got_ref, low_ref, high_ref, keep_ref)


def cross_of(keep_ref, came_ref, own_bf, other_bf):
    return lax.dot_general(
        keep_ref[...], template_pair(own_bf), NT, preferred_element_type=F32
    ) + lax.dot_general(
        came_ref[...], template_pair(other_bf), NT, preferred_element_type=F32
    )


def spread(value, lane):
    width = value.shape[1]
    wide = jnp.concatenate(
        [value, jnp.zeros((value.shape[0], LANES - width), F32)], axis=1
    )
    return wide if lane == 0 else pltpu.roll(wide, lane, 1)


def pack_gram(gram):
    top = spread(gram[0:16, :], 0) + spread(gram[16:32, :], 64)
    corner = gram[32:64, 32:64]
    low = sum(spread(corner[8 * i:8 * i + 8, :], 32 * i) for i in range(4))
    return jnp.concatenate([top, low], axis=0)


def unpack_gram(packed):
    top = jnp.concatenate(
        [packed[0:16, :], pltpu.roll(packed[0:16, :], 64, 1)], axis=0
    )[:, 0:RANK]
    low = packed[16:24, :]
    corner = jnp.concatenate(
        [low] + [pltpu.roll(low, LANES - 32 * i, 1) for i in range(1, 4)], axis=0
    )
    side = pad_to(top, LANES, LANES).T[32:64, :]
    lane = lax.broadcasted_iota(jnp.int32, (32, LANES), 1)
    bottom = jnp.where(lane < 32, side, pltpu.roll(corner, 32, 1))
    return jnp.concatenate([top, bottom[:, 0:RANK]], axis=0)


def exact(left, right):
    return jnp.dot(left, right, precision=lax.Precision.HIGHEST, preferred_element_type=F32)


def descend(state, residual, gram):
    eye = lax.broadcasted_iota(jnp.int32, (RANK, RANK), 0) == lax.broadcasted_iota(
        jnp.int32, (RANK, RANK), 1
    )
    pivot = jnp.sum(jnp.where(eye, gram, 0.0), axis=1, keepdims=True) + EPSILON
    inverse = 1.0 / pivot
    goal = state + residual * inverse
    scaled = gram * inverse
    goals = [goal[8 * i:8 * i + 8, :] for i in range(8)]
    done = []
    for k in range(RANK):
        old = state[k:k + 1, :]
        new = jnp.maximum(goals[k // 8][k % 8:k % 8 + 1, :], 0.0)
        done.append(new)
        change = new - old
        for i in range(k // 8, 8):
            goals[i] = goals[i] - scaled[8 * i:8 * i + 8, k:k + 1] * change
    return jnp.concatenate(done, axis=0)


def pad_to(value, rows, lanes):
    if value.shape[1] < lanes:
        value = jnp.concatenate(
            [value, jnp.zeros((value.shape[0], lanes - value.shape[1]), F32)], axis=1
        )
    if value.shape[0] < rows:
        value = jnp.concatenate(
            [value, jnp.zeros((rows - value.shape[0], value.shape[1]), F32)], axis=0
        )
    return value


def activation_body(first, *refs):
    if first:
        cross_ref, gram_ref, state_ref, new_ref, out_ref = refs
    else:
        cross_ref, state_ref, new_ref, out_ref = refs
    total = jnp.sum(cross_ref[...].astype(F32), axis=0)
    cross = pad_to(total[0:16, :], LANES, LANES).T
    wanted = cross[0:64, :] + pltpu.roll(cross[64:128, :], 16, 1)
    gram = unpack_gram(gram_ref[...] if first else total[16:40, :])
    if first:
        state = pad_to(state_ref[...], LANES, LANES).T[0:RANK, :]
    else:
        state = state_ref[...]
    rest = state if first else state - state.astype(BF).astype(F32)
    updated = descend(state, wanted - exact(gram, rest), gram)
    new_ref[...] = updated
    both = jnp.concatenate([updated, pltpu.roll(updated, LANES - 16, 1)], axis=0).T
    out_ref[...] = jnp.broadcast_to(both[0:16, :].astype(BF)[None], out_ref.shape)


def plain_gram(packed):
    return jnp.concatenate(
        [packed[:, 0:RANK], pltpu.roll(packed, RANK, 1)[:, 0:RANK]], axis=0
    )


def project(activ, spectra):
    proj = lax.dot_general(activ, spectra, TN, preferred_element_type=F32)
    return proj[0:64, 0:LANES] + proj[64:128, LANES:]


def activ_gram(activ):
    gram = lax.dot_general(activ, activ, TN, preferred_element_type=F32)
    gram = gram[0:64, 0:64] + pltpu.roll(gram[64:128, :], 64, 1)[:, 0:64]
    return spread(gram[0:32, :], 0) + spread(gram[32:64, :], 64)


def project_body(activ_ref, keep_ref, came_ref, own_ref, send_ref):
    activ = activ_ref[...]
    gram = activ_gram(activ)
    own, other = project(activ, keep_ref[...]), project(activ, came_ref[...])
    own_ref[0:32, :] = gram
    own_ref[32:96, :] = own
    own_ref[96:160, :] = other
    send_ref[0:32, :] = gram
    send_ref[32:96, :] = other
    send_ref[96:160, :] = own


def own_project_body(activ_ref, keep_ref, out_ref):
    activ = activ_ref[...]
    out_ref[0:32, :] = activ_gram(activ)
    out_ref[32:96, :] = project(activ, keep_ref[...])


def add_project_body(activ_ref, away_ref, part_ref, out_ref):
    activ = activ_ref[...]
    out_ref[0:32, :] = part_ref[0:32, :] + activ_gram(activ)
    out_ref[32:96, :] = part_ref[32:96, :] + project(activ, away_ref[...])


def new_templates(part_refs, templ):
    one, two, three, four = (ref[...] for ref in part_refs)
    total = (one + three) + (two + four)
    gram, proj = plain_gram(total[0:32, :]), total[32:96, :]
    if total.shape[0] > 96:
        proj = jnp.concatenate([proj, total[96:160, :]], axis=1)
    return descend(templ, proj - exact(gram, templ), gram)


def template_body(a_ref, b_ref, c_ref, d_ref, own_ref, other_ref, activ_ref, keep_ref, came_ref, new_ref, out_ref):
    templ = jnp.concatenate([own_ref[...], other_ref[...]], axis=1)
    updated = new_templates((a_ref, b_ref, c_ref, d_ref), templ)
    new_ref[...] = updated[:, 0:LANES]
    templ_bf = updated.astype(BF)
    full = lax.dot_general(templ_bf, templ_bf, NT, preferred_element_type=F32)
    square = template_pair(full)
    high = square.astype(BF)
    low = (square - high.astype(F32)).astype(BF)
    rows = activ_ref[...]
    fitted = jnp.dot(rows, high, preferred_element_type=F32) + jnp.dot(
        rows, low, preferred_element_type=F32
    )
    cross = cross_of(keep_ref, came_ref, templ_bf[:, 0:LANES], templ_bf[:, LANES:]) - fitted
    gram = jnp.broadcast_to(pack_gram(full)[None], (32, 24, LANES))
    out_ref[...] = jnp.concatenate([cross.reshape(32, 16, LANES), gram], axis=1).astype(BF)


def last_template_body(a_ref, b_ref, c_ref, d_ref, templ_ref, state_ref, new_ref, activ_ref):
    activ_ref[...] = pad_to(state_ref[...], LANES, LANES).T[0:32, 0:RANK]
    updated = new_templates((a_ref, b_ref, c_ref, d_ref), templ_ref[...])
    new_ref[...] = updated[:, 0:PIX]


def first_gram_body(templ_ref, gram_ref):
    templ_bf = templ_ref[...].astype(BF)
    gram_ref[...] = pack_gram(
        lax.dot_general(templ_bf, templ_bf, NT, preferred_element_type=F32)
    )


def shift(value, axis, size, by):
    return lax.ppermute(value, axis, [(i, (i + by) % size) for i in range(size)])


def ring_sum(value, axis, size, step):
    return (value + shift(value, axis, size, 2 * step)) + (
        shift(value, axis, size, step) + shift(value, axis, size, 3 * step)
    )


def from_ahead(value, by):
    pairs = [
        ((z + 4 * c + by) % NZ * NC + c, z * NC + c) for z in range(NZ) for c in range(NC)
    ]
    return lax.ppermute(value, ("z", "c"), pairs)


def near(part):
    part = ring_sum(part + shift(part, "c", NC, 1), "x", NX, 1)
    return sum(from_ahead(part, by) for by in range(4))


def first_message_body(own_ref, other_ref, keep_ref, came_ref, out_ref):
    cross = cross_of(keep_ref, came_ref, own_ref[...].astype(BF), other_ref[...].astype(BF))
    out_ref[...] = cross.reshape(32, 16, LANES)


def sds(*shape, dtype=F32):
    return jax.ShapeDtypeStruct(shape, dtype)


def shards(flux, ivar, row_target, start_w, start_h):
    core = lax.axis_index("c").astype(jnp.int32).reshape(1)
    send = pack(flux, ivar, row_target.reshape(1, ROWS))
    templates = jnp.pad(start_h, ((0, 0), (0, LANES - PIX)))
    got = lax.all_to_all(send, TGT, split_axis=0, concat_axis=0, tiled=True)
    gram = near(call(first_gram_body, sds(24, LANES), (templates,)))
    other = shift(templates, "c", NC, 1)
    got, gram, other = lax.optimization_barrier((got, gram, other))
    gram = gram + shift(gram, "c", NC, 1)
    rows = got.reshape(N_TGT * ROWS, 2 * LANES)
    half = sds(512, 2 * LANES, dtype=BF)
    cost = 2 * 1024 * N_TGT * ROWS * 2 * LANES
    away, low, high = call(
        away_body,
        (half, sds(64, N_TGT * ROWS, dtype=BF), sds(8, N_TGT * ROWS)),
        (core, rows),
        scalars=1,
        flops=cost,
    )
    came = shift(away, "c", NC, 1)
    keep = call(keep_body, half, (core, rows, low, high), scalars=1, flops=cost)
    cross = call(
        first_message_body, sds(32, 16, LANES), (templates, other, keep, came)
    )
    cross, gram = lax.optimization_barrier((cross, gram))
    state = start_w
    for sweep in range(SWEEPS):
        first = sweep == 0
        cross = lax.all_to_all(cross, ("x", "z"), split_axis=0, concat_axis=0, tiled=True)
        state, message = call(
            lambda *refs, first=first: activation_body(first, *refs),
            (sds(RANK, LANES), sds(32, 16, LANES, dtype=BF)),
            (cross, gram, state) if first else (cross, state),
        )
        activ = lax.all_to_all(message, ("x", "z"), split_axis=0, concat_axis=0, tiled=True)
        activ = activ.reshape(512, LANES)
        if first:
            both = (sds(160, LANES), sds(160, LANES))
            part, sent = call(project_body, both, (activ, keep, came))
            part = part + shift(sent, "c", NC, 1)
        else:
            came_activ = shift(activ, "c", NC, 1)
            part = call(
                own_project_body, sds(96, LANES), (activ, keep), flops=2 * 128 * 512 * 384
            )
            part = call(add_project_body, sds(96, LANES), (came_activ, away, part))
        parts = (part, *(shift(part, "y", NY, by) for by in (1, 2, 3)))
        if first:
            templates, cross = call(
                template_body,
                (sds(RANK, LANES), sds(32, 40, LANES, dtype=BF)),
                (*parts, templates, other, activ, keep, came),
            )
        else:
            templates, state = call(
                last_template_body,
                (sds(RANK, PIX), sds(32, RANK)),
                (*parts, templates, state),
            )
    return state, templates


def solution(mesh):
    grid = Mesh(mesh.devices.reshape(NX, NZ, NC, NY), ("x", "z", "c", "y"))
    every = ("x", "z", "c", "y")
    return jax.shard_map(
        shards,
        mesh=grid,
        in_specs=(P(every, None), P(every, None), P(every), P(every, None), P(None, TGT)),
        out_specs=(P(every, None), P(None, TGT)),
        check_vma=False,
    )
```
